32 devices in a mesh: tm: 4 (over z), space: 4 (over x, core), node: 2 (over y).
Axes of the slice: x: 2, y: 2, z: 4, core: 2. Of those that a mesh axis runs over, the one named last changes fastest.
Arguments:
- initial: float32 [8, 64, 256], P(None, 'space'), may hold values from -6 to 6
- forcing: float32 [4, 8, 64, 256], P('tm', None, 'space'), may hold values from -6 to 6
- decay_rate: float32 [8, 64, 256], P(None, 'space'), may hold values from 0.02 to 20
- mixing: float32 [8, 8], replicated, may hold values from -2 to 2
- diffusivity: float32 [8], replicated, may hold values from 0.3 to 2
- velocity: float32 [3, 8], replicated, may hold values from -2 to 2
Outputs:
- node_values: float32 [4, 2, 8, 64, 256], P('tm', 'node', None, 'space')
The draws below stay inside these ranges and needn't reach their ends.
All inputs are finite; a program needn't handle non-finite values.
Results may differ from the reference program's by a relative error of at most 0.0003.
Values sent between devices are 32-bit elements; how exact they have to be, the bound alone decides.
A program may use at most 64 MiB of HBM per device.

```python
import math
import jax
import jax.numpy as jnp
import numpy as np
from jax import lax

S = 8
NY = 16
NZ = 16
NX = 64
SLICES = 4
N_NODE = 2


def shard_levels(key, shape, pieces, least, top_value):
    loudness = 1.0
    for dim, parts in pieces:
        draws = jax.random.uniform(jax.random.fold_in(jax.random.fold_in(key, 6), dim), (parts,), jnp.float32, least / len(pieces), top_value / len(pieces))
        loudness = loudness * jnp.repeat(jnp.exp(draws), shape[dim] // parts).reshape((-1,) + (1,) * (len(shape) - 1 - dim))
    return loudness


def gaussian(rng, shape, deviation, reach, split=(), dtype=jnp.bfloat16):
    entries = jax.random.normal(rng, shape, jnp.float32) * deviation
    if len(split) > 0:
        entries = shard_levels(rng, shape, split, -0.22, 0.18) * entries
    return jnp.clip(entries, min=-reach, max=reach).astype(dtype)


def setup_inputs(seed: int = 0) -> dict:
    streams_of = jax.random.split(jax.random.key(seed), 7)
    initial = gaussian(streams_of[0], (S, NX, NY * NZ), 1.0, 6.0, ((1, 4),), jnp.float32)
    forcing = gaussian(streams_of[1], (SLICES, S, NX, NY * NZ), 1.0, 6.0, ((0, 4), (2, 4)), jnp.float32)
    decay_rate = jnp.clip(jnp.exp(math.log(20.0) - 6.9077553 * jax.random.uniform(streams_of[2], (S, NX, NY * NZ), jnp.float32) ** shard_levels(streams_of[2], (S, NX, NY * NZ), ((1, 4),), -0.2, 0.2)), 0.02, 20.0)
    mixing = gaussian(streams_of[3], (S, S), S ** -0.5, 2.0, (), jnp.float32)
    diffusivity = jnp.clip(jnp.exp(jax.random.uniform(streams_of[4], (S,), jnp.float32, math.log(0.3), math.log(2.0))), 0.3, 2.0)
    velocity = jnp.clip(jax.random.uniform(streams_of[5], (3, S), jnp.float32, -2.0, 2.0), -2.0, 2.0)
    return dict(initial=initial, forcing=forcing, decay_rate=decay_rate, mixing=mixing, diffusivity=diffusivity, velocity=velocity)


time_step = 0.05


def quadrature(node_count):
    points = [(position + 1.0) / node_count for position in range(node_count)]
    weights_table = np.zeros((node_count, node_count))
    for column in range(node_count):
        coeffs = [1.0]
        denominator = 1.0
        for other_node in range(node_count):
            if other_node != column:
                shifted = [0.0] + coeffs
                for degree in range(len(coeffs)):
                    shifted[degree] = shifted[degree] - points[other_node] * coeffs[degree]
                coeffs = shifted
                denominator = denominator * (points[column] - points[other_node])
        for row_node in range(node_count):
            running = 0.0
            for degree in range(len(coeffs)):
                running = running + coeffs[degree] * points[row_node] ** (degree + 1) / (degree + 1)
            weights_table[row_node, column] = running / denominator
    return weights_table, np.array(points)


def rate_of(padded, decay_rate, mixing, diffusivity, velocity, force_now):
    center = padded[:, 1:-1]
    x_plus = padded[:, 2:]
    x_minus = padded[:, :-2]
    y_plus = jnp.roll(center, -NZ, axis=2)
    y_minus = jnp.roll(center, NZ, axis=2)
    depth_index = jnp.arange(center.shape[2]) % NZ
    z_plus = jnp.where(depth_index == NZ - 1, 0.0, jnp.roll(center, -1, axis=2))
    z_minus = jnp.where(depth_index == 0, 0.0, jnp.roll(center, 1, axis=2))
    laplace = (x_plus + x_minus) + (y_plus + y_minus) + (z_plus + z_minus) - 6.0 * center
    drift_term = (velocity[0][:, None, None] * (x_plus - x_minus)
                  + velocity[1][:, None, None] * (y_plus - y_minus)
                  + velocity[2][:, None, None] * (z_plus - z_minus))
    coupled = jnp.tanh(jnp.einsum("ts,sxc->txc", mixing, center, precision=lax.Precision.HIGHEST))
    return diffusivity[:, None, None] * laplace - 0.5 * drift_term - decay_rate * center + coupled + force_now


def reference(initial, forcing, decay_rate, mixing, diffusivity, velocity):
    weights_table, points = quadrature(N_NODE)
    q_table = jnp.asarray(weights_table, jnp.float32)
    node_time = jnp.asarray(points, jnp.float32)[:, None, None, None]
    stiff_part = time_step * (node_time / N_NODE) * decay_rate[None]
    factor = 1.0 / (1.0 + time_step * decay_rate)

    def advance(carried, force_now):
        return factor * carried + time_step * force_now * factor, carried

    _, starts = lax.scan(advance, initial, forcing)

    def first_nodes(slice_start, force_now):
        return (slice_start[None] + node_time * time_step * force_now[None]) / (1.0 + node_time * time_step * decay_rate[None])

    def sweep_nodes(slice_start, nodes_now, force_now):
        def one_rate(field_now):
            padded = jnp.pad(field_now, ((0, 0), (1, 1), (0, 0)))
            return rate_of(padded, decay_rate, mixing, diffusivity, velocity, force_now)

        node_rates = jax.vmap(one_rate)(nodes_now)
        summed = jnp.einsum("mj,jsxc->msxc", q_table, node_rates, precision=lax.Precision.HIGHEST)
        return (slice_start[None] + time_step * summed + stiff_part * nodes_now) / (1.0 + stiff_part)

    def slice_end(inputs_now):
        slice_start, force_now = inputs_now
        return sweep_nodes(slice_start, first_nodes(slice_start, force_now), force_now)[-1]

    ends = lax.map(slice_end, (starts, forcing))
    handed = jnp.concatenate([initial[None], ends[:-1]], axis=0)

    def slice_final(inputs_now):
        slice_start, second_start, force_now = inputs_now
        first_pass = sweep_nodes(slice_start, first_nodes(slice_start, force_now), force_now)
        return sweep_nodes(second_start, first_pass, force_now)

    return lax.map(slice_final, (starts, handed, forcing))
```

```python
import functools

import jax
import jax.numpy as jnp
import numpy as np
from jax import lax
from jax.experimental import pallas as pl
from jax.experimental.pallas import tpu as pltpu
from jax.sharding import PartitionSpec as P

NZ = 16
WIDTH = 2
TILE = 8

time_step = 0.05


def quadrature(node_count):
    points = [(position + 1.0) / node_count for position in range(node_count)]
    weights_table = np.zeros((node_count, node_count))
    for column in range(node_count):
        coeffs = [1.0]
        denominator = 1.0
        for other_node in range(node_count):
            if other_node != column:
                shifted = [0.0] + coeffs
                for degree in range(len(coeffs)):
                    shifted[degree] = shifted[degree] - points[other_node] * coeffs[degree]
                coeffs = shifted
                denominator = denominator * (points[column] - points[other_node])
        for row_node in range(node_count):
            running = 0.0
            for degree in range(len(coeffs)):
                running = running + coeffs[degree] * points[row_node] ** (degree + 1) / (degree + 1)
            weights_table[row_node, column] = running / denominator
    return (weights_table, np.array(points))


def kernel(
    slices, pieces, nodes,
    initial_hbm, forcing_hbm, decay_hbm, mix, diff, vel, out_hbm,
    start, force, decay, handed, following, grow, shift,
    node_inv, node_add, sweep_inv, own_inv,
    field, mixed, base, last_value, result,
    side_send, side_recv, edge_send, edge_first, edge_recv,
    load_sem, out_sem,
    side_ss, side_rs, edge_ss, first_ss, edge_rs, start_ss, start_rs, hand_ss, hand_rs,
):
    species, rows, cells = following.shape
    tiles = rows // TILE
    halo = slice(rows, rows + TILE)
    h = time_step
    table, points = quadrature(nodes)
    n = lax.axis_index("tm")
    p = lax.axis_index("space")
    m = lax.axis_index("node")
    has_left, has_right = p > 0, p < pieces - 1
    has_before, has_after = n > 0, n < slices - 1
    sides = ((has_left, p - 1), (has_right, p + 1))
    mesh_id = pl.DeviceIdType.MESH

    barrier = pltpu.get_barrier_semaphore()

    def greet(condition, where):
        @pl.when(condition)
        def _():
            pl.semaphore_signal(barrier, inc=1, device_id=where, device_id_type=mesh_id)

    greet(has_before, {"tm": n - 1})
    for present, place in sides:
        greet(present, {"space": place})
        greet(present & has_before, {"tm": n - 1, "space": place})

    load_force = pltpu.make_async_copy(forcing_hbm.at[0], force.at[:, 0:rows], load_sem.at[0])
    load_decay = pltpu.make_async_copy(decay_hbm, decay.at[:, 0:rows], load_sem.at[1])
    load_start = pltpu.make_async_copy(initial_hbm, start.at[:, 0:rows], load_sem.at[2])
    load_handed = pltpu.make_async_copy(initial_hbm, handed, load_sem.at[3])
    load_force.start()
    load_decay.start()

    @pl.when(n == 0)
    def _():
        load_start.start()
        load_handed.start()

    zero_tile = jnp.zeros((species, TILE, cells), jnp.float32)
    start[:, halo, :] = zero_tile
    force[:, halo, :] = zero_tile
    decay[:, halo, :] = zero_tile

    def send(src, dst, ss, rs, where):
        return pltpu.make_async_remote_copy(
            src_ref=src, dst_ref=dst, send_sem=ss, recv_sem=rs, device_id=where, device_id_type=mesh_id
        )

    def side_copy(k):
        return send(side_send.at[k], side_recv.at[1 - k], side_ss.at[k], side_rs.at[1 - k], {"space": sides[k][1]})

    def first_copy(k):
        return send(edge_first.at[k], edge_recv.at[1 - k], first_ss.at[k], edge_rs.at[1 - k], {"space": sides[k][1]})

    def edge_copy(k):
        return send(
            edge_send.at[k], edge_recv.at[1 - k], edge_ss.at[k], edge_rs.at[1 - k],
            {"tm": n + 1, "space": sides[k][1]},
        )

    def start_copy(s):
        return send(following.at[s], start.at[s, 0:rows], start_ss.at[s], start_rs.at[s], {"tm": n + 1})

    def hand_copy(t):
        part = pl.ds(TILE * t, TILE)
        return send(last_value.at[:, part], handed.at[:, part], hand_ss.at[t], hand_rs.at[t], {"tm": n + 1})

    def pack(dst, offset, src, s):
        low = offset + WIDTH * s
        dst[0, low:low + WIDTH, :] = src[s, 0:WIDTH, :]
        dst[1, low:low + WIDTH, :] = src[s, rows - WIDTH:rows, :]

    def unpack(dst, src, k, offset):
        for s in range(species):
            low = offset + WIDTH * s
            if k == 0:
                dst[s, rows + TILE - WIDTH:rows + TILE, :] = src[0, low:low + WIDTH, :]
            else:
                dst[s, rows:rows + WIDTH, :] = src[1, low:low + WIDTH, :]

    load_force.wait()
    load_decay.wait()
    whole = slice(0, rows)
    for s in range(species):
        inverse = 1.0 / (1.0 + h * decay[s, whole, :])
        grow[s] = inverse
        shift[s] = h * force[s, whole, :] * inverse
        pack(side_send, 0, force, s)
        pack(side_send, WIDTH * species, decay, s)

    def present_count(flag):
        return flag.astype(jnp.int32)

    beside = present_count(has_left) + present_count(has_right)
    pl.semaphore_wait(barrier, beside + present_count(has_after) * (1 + beside))

    def pass_on(s):
        following[s] = grow[s] * start[s, whole, :] + shift[s]

        @pl.when(has_after)
        def _():
            start_copy(s).start()

        pack(edge_send, 0, following, s)

    def pass_edges():
        for k in range(2):
            @pl.when(has_after & sides[k][0])
            def _():
                edge_copy(k).start()

    @pl.when(n == 0)
    def _():
        load_start.wait()
        for s in range(species):
            pass_on(s)
        pass_edges()
        for s in range(species):
            pack(edge_first, 0, start, s)
        for k in range(2):
            @pl.when(sides[k][0])
            def _():
                first_copy(k).start()

    for k in range(2):
        @pl.when(sides[k][0])
        def _():
            side_copy(k).start()

    own_time = jnp.float32(0.0)
    own_row = [jnp.float32(0.0)] * nodes
    for i in range(nodes):
        own_time = jnp.where(m == i, jnp.float32(points[i]), own_time)
        own_row = [jnp.where(m == i, jnp.float32(table[i, j]), own_row[j]) for j in range(nodes)]
    own_stiff = own_time * jnp.float32(h / nodes)

    def prepare(s, part):
        d = decay[s, part, :]
        f = force[s, part, :]
        for j in range(nodes):
            inverse = 1.0 / (1.0 + float(points[j] * h) * d)
            node_inv[j, s, part, :] = inverse
            node_add[j, s, part, :] = float(points[j] * h) * f * inverse
            sweep_inv[j, s, part, :] = 1.0 / (1.0 + float(h * points[j] / nodes) * d)

    for s in range(species):
        prepare(s, whole)
        own_inv[s] = 1.0 / (1.0 + own_stiff * decay[s, whole, :])
    for k in range(2):
        @pl.when(sides[k][0])
        def _():
            side_copy(1 - k).wait_recv()
            unpack(force, side_recv, k, 0)
            unpack(decay, side_recv, k, WIDTH * species)
    for s in range(species):
        prepare(s, halo)

    def node_values(s, part):
        w = start[s, part, :]
        return [w * node_inv[j, s, part, :] + node_add[j, s, part, :] for j in range(nodes)]

    def interior_values(s):
        values = node_values(s, whole)
        for j in range(nodes):
            field[j, s, TILE:TILE + rows, :] = values[j]
            field[j, s, 2 * TILE + rows:3 * TILE + rows, :] = values[j][0:TILE]

    @pl.when(n == 0)
    def _():
        for s in range(species):
            interior_values(s)

    @pl.when(has_before)
    def _():
        for s in range(species):
            start_copy(s).wait_recv()
            pass_on(s)
            interior_values(s)
        pass_edges()

    for k in range(2):
        @pl.when(sides[k][0])
        def _():
            edge_copy(1 - k).wait_recv()
            unpack(start, edge_recv, k, 0)
    for s in range(species):
        values = node_values(s, halo)
        for j in range(nodes):
            field[j, s, 0:TILE, :] = values[j]
            field[j, s, TILE + rows:2 * TILE + rows, :] = values[j]

    depth = lax.broadcasted_iota(jnp.int32, (TILE, cells), 1) % NZ
    is_first, is_last = depth == 0, depth == NZ - 1
    row = lax.broadcasted_iota(jnp.int32, (TILE, cells), 0)
    inside = ((row < WIDTH) & has_right) | ((row >= TILE - WIDTH) & has_left)

    def linear(ref, s, low, d):
        c = ref[s, low:low + TILE, :]
        x_plus = ref[s, low + 1:low + TILE + 1, :]
        x_minus = ref[s, low - 1:low + TILE - 1, :]
        y_plus = pltpu.roll(c, cells - NZ, 1)
        y_minus = pltpu.roll(c, NZ, 1)
        z_plus = jnp.where(is_last, 0.0, pltpu.roll(c, cells - 1, 1))
        z_minus = jnp.where(is_first, 0.0, pltpu.roll(c, 1, 1))
        dd = diff[s]
        vx, vy, vz = 0.5 * vel[0, s], 0.5 * vel[1, s], 0.5 * vel[2, s]
        return (
            ((dd - vx) * x_plus + (dd + vx) * x_minus)
            + ((dd - vy) * y_plus + (dd + vy) * y_minus)
            + ((dd - vz) * z_plus + (dd + vz) * z_minus)
            - (6.0 * dd + d) * c
        )

    def coupled(values, s):
        total = mix[s, 0] * values[0]
        for t in range(1, species):
            total = total + mix[s, t] * values[t]
        return jnp.tanh(total)

    for t in list(range(tiles)) + [tiles]:
        part = slice(TILE * t, TILE * t + TILE)
        low = TILE * (t + 1)
        is_halo = t == tiles
        fresh = [[None] * species for _ in range(nodes)]
        centers = [[field[j, s, low:low + TILE, :] for s in range(species)] for j in range(nodes)]
        for s in range(species):
            d = decay[s, part, :]
            f = force[s, part, :]
            w = start[s, part, :]
            rates = [linear(field.at[j], s, low, d) + coupled(centers[j], s) + f for j in range(nodes)]
            for i in range(nodes):
                total = float(h * table[i, 0]) * rates[0]
                for j in range(1, nodes):
                    total = total + float(h * table[i, j]) * rates[j]
                v = (w + total + float(h * points[i] / nodes) * d * centers[i][s]) * sweep_inv[i, s, part, :]
                fresh[i][s] = jnp.where(inside, v, 0.0) if is_halo else v
            if not is_halo:
                last_value[s, part, :] = fresh[nodes - 1][s]
            sum_now = own_row[0] * fresh[0][s]
            for j in range(1, nodes):
                sum_now = sum_now + own_row[j] * fresh[j][s]
            mixed[s, low:low + TILE, :] = sum_now
            if is_halo:
                mixed[s, 0:TILE, :] = sum_now
        if not is_halo:
            @pl.when(has_after)
            def _():
                hand_copy(t).start()

            for s in range(species):
                gained = own_time * force[s, part, :]
                own = fresh[0][s]
                for j in range(nodes):
                    gained = gained + own_row[j] * coupled(fresh[j], s)
                    if j > 0:
                        own = jnp.where(m == j, fresh[j][s], own)
                base[s, part, :] = h * gained + own_stiff * decay[s, part, :] * own

    for t in range(tiles):
        part = slice(TILE * t, TILE * t + TILE)
        for s in range(species):
            rate = linear(mixed, s, TILE * (t + 1), decay[s, part, :])
            base[s, part, :] = (base[s, part, :] + h * rate) * own_inv[s, part, :]

    @pl.when(n == 0)
    def _():
        load_handed.wait()

    def out_copy(t):
        part = pl.ds(TILE * t, TILE)
        return pltpu.make_async_copy(result.at[:, part], out_hbm.at[0, 0, :, part], out_sem.at[t])

    for t in range(tiles):
        part = slice(TILE * t, TILE * t + TILE)

        @pl.when(has_before)
        def _():
            hand_copy(t).wait_recv()

        result[:, part, :] = handed[:, part, :] * own_inv[:, part, :] + base[:, part, :]
        out_copy(t).start()

    for k in range(2):
        @pl.when(sides[k][0])
        def _():
            side_copy(k).wait_send()

        @pl.when(sides[k][0] & (n == 0))
        def _():
            first_copy(k).wait_send()

        @pl.when(sides[k][0] & has_after)
        def _():
            edge_copy(k).wait_send()

    @pl.when(has_after)
    def _():
        for s in range(species):
            start_copy(s).wait_send()
        for t in range(tiles):
            hand_copy(t).wait_send()

    for t in range(tiles):
        out_copy(t).wait()


def body(initial, forcing, decay_rate, mixing, diffusivity, velocity):
    slices, pieces, nodes = (lax.axis_size(a) for a in ("tm", "space", "node"))
    species, rows, cells = initial.shape
    longer = rows + TILE
    packed = WIDTH * species
    tiles = rows // TILE
    f32 = jnp.float32
    dma = pltpu.SemaphoreType.DMA
    hbm = pl.BlockSpec(memory_space=pl.ANY)
    smem = pl.BlockSpec(memory_space=pltpu.SMEM)
    plain = pltpu.VMEM((species, rows, cells), f32)
    extended = pltpu.VMEM((species, longer, cells), f32)
    per_node = pltpu.VMEM((nodes, species, longer, cells), f32)
    return pl.pallas_call(
        functools.partial(kernel, slices, pieces, nodes),
        out_shape=jax.ShapeDtypeStruct((1, 1, species, rows, cells), f32),
        in_specs=[hbm, hbm, hbm, smem, smem, smem],
        out_specs=hbm,
        scratch_shapes=[
            extended, extended, extended, plain, plain, plain, plain,
            per_node, per_node, per_node, plain,
            pltpu.VMEM((nodes, species, rows + 3 * TILE, cells), f32),
            pltpu.VMEM((species, rows + 2 * TILE, cells), f32),
            plain, plain, plain,
            pltpu.VMEM((2, 2 * packed, cells), f32),
            pltpu.VMEM((2, 2 * packed, cells), f32),
            pltpu.VMEM((2, packed, cells), f32),
            pltpu.VMEM((2, packed, cells), f32),
            pltpu.VMEM((2, packed, cells), f32),
            dma((4,)), dma((tiles,)),
            dma((2,)), dma((2,)), dma((2,)), dma((2,)), dma((2,)),
            dma((species,)), dma((species,)), dma((tiles,)), dma((tiles,)),
        ],
        compiler_params=pltpu.CompilerParams(
            collective_id=0, has_side_effects=True, vmem_limit_bytes=60 * 1024 * 1024
        ),
    )(initial, forcing, decay_rate, mixing, diffusivity, velocity)


def solution(mesh):
    placed = (
        P(None, "space", None),
        P("tm", None, "space", None),
        P(None, "space", None),
        P(),
        P(),
        P(),
    )
    return jax.shard_map(
        body,
        mesh=mesh,
        in_specs=placed,
        out_specs=P("tm", "node", None, "space", None),
        check_vma=False,
    )
```

```python
import functools

import jax
import jax.numpy as jnp
import numpy as np
from jax import lax
from jax.experimental import pallas as pl
from jax.experimental.pallas import tpu as pltpu
from jax.sharding import PartitionSpec as P

NZ = 16
WIDTH = 2
TILE = 8

time_step = 0.05


def quadrature(node_count):
    points = [(position + 1.0) / node_count for position in range(node_count)]
    weights_table = np.zeros((node_count, node_count))
    for column in range(node_count):
        coeffs = [1.0]
        denominator = 1.0
        for other_node in range(node_count):
            if other_node != column:
                shifted = [0.0] + coeffs
                for degree in range(len(coeffs)):
                    shifted[degree] = shifted[degree] - points[other_node] * coeffs[degree]
                coeffs = shifted
                denominator = denominator * (points[column] - points[other_node])
        for row_node in range(node_count):
            running = 0.0
            for degree in range(len(coeffs)):
                running = running + coeffs[degree] * points[row_node] ** (degree + 1) / (degree + 1)
            weights_table[row_node, column] = running / denominator
    return (weights_table, np.array(points))


def kernel(
    slices, pieces, nodes,
    initial_hbm, forcing_hbm, decay_hbm, mix_hbm, diff_hbm, vel_hbm, out_ref,
    mix, diff, vel, start, force, decay, handed, following, grow, shift,
    node_inv, node_add, sweep_inv, own_inv,
    field, mixed, base, last_value,
    side_send, side_recv, edge_send, edge_first, edge_recv,
    load_sem,
    side_ss, side_rs, edge_ss, first_ss, edge_rs, start_ss, start_rs, hand_ss, hand_rs,
):
    species, rows, cells = following.shape
    tiles = rows // TILE
    halo = slice(rows, rows + TILE)
    h = time_step
    table, points = quadrature(nodes)
    n = lax.axis_index("tm")
    p = lax.axis_index("space")
    m = lax.axis_index("node")
    has_left, has_right = p > 0, p < pieces - 1
    has_before, has_after = n > 0, n < slices - 1
    sides = ((has_left, p - 1), (has_right, p + 1))
    mesh_id = pl.DeviceIdType.MESH

    barrier = pltpu.get_barrier_semaphore()

    def greet(condition, where):
        @pl.when(condition)
        def _():
            pl.semaphore_signal(barrier, inc=1, device_id=where, device_id_type=mesh_id)

    greet(has_before, {"tm": n - 1})
    for present, place in sides:
        greet(present, {"space": place})
        greet(present & has_before, {"tm": n - 1, "space": place})

    load_force = pltpu.make_async_copy(forcing_hbm.at[0], force.at[:, 0:rows], load_sem.at[0])
    load_decay = pltpu.make_async_copy(decay_hbm, decay.at[:, 0:rows], load_sem.at[1])
    load_start = pltpu.make_async_copy(initial_hbm, start.at[:, 0:rows], load_sem.at[2])
    load_handed = pltpu.make_async_copy(initial_hbm, handed, load_sem.at[3])
    loads = [
        pltpu.make_async_copy(src, dst, load_sem.at[4 + i])
        for i, (src, dst) in enumerate([(mix_hbm, mix), (diff_hbm, diff), (vel_hbm, vel)])
    ]
    load_force.start()
    load_decay.start()
    for load in loads:
        load.start()

    @pl.when(n == 0)
    def _():
        load_start.start()
        load_handed.start()

    zero_tile = jnp.zeros((species, TILE, cells), jnp.float32)
    start[:, halo, :] = zero_tile
    force[:, halo, :] = zero_tile
    decay[:, halo, :] = zero_tile

    def send(src, dst, ss, rs, where):
        return pltpu.make_async_remote_copy(
            src_ref=src, dst_ref=dst, send_sem=ss, recv_sem=rs, device_id=where, device_id_type=mesh_id
        )

    def side_copy(k):
        return send(side_send.at[k], side_recv.at[1 - k], side_ss.at[k], side_rs.at[1 - k], {"space": sides[k][1]})

    def first_copy(k):
        return send(edge_first.at[k], edge_recv.at[1 - k], first_ss.at[k], edge_rs.at[1 - k], {"space": sides[k][1]})

    def edge_copy(k):
        return send(
            edge_send.at[k], edge_recv.at[1 - k], edge_ss.at[k], edge_rs.at[1 - k],
            {"tm": n + 1, "space": sides[k][1]},
        )

    def start_copy(s):
        return send(following.at[s], start.at[s, 0:rows], start_ss.at[s], start_rs.at[s], {"tm": n + 1})

    def hand_copy(t):
        part = pl.ds(TILE * t, TILE)
        return send(last_value.at[:, part], handed.at[:, part], hand_ss.at[t], hand_rs.at[t], {"tm": n + 1})

    def pack(dst, offset, src, s):
        low = offset + WIDTH * s
        dst[0, low:low + WIDTH, :] = src[s, 0:WIDTH, :]
        dst[1, low:low + WIDTH, :] = src[s, rows - WIDTH:rows, :]

    def unpack(dst, src, k, offset):
        for s in range(species):
            low = offset + WIDTH * s
            if k == 0:
                dst[s, rows + TILE - WIDTH:rows + TILE, :] = src[0, low:low + WIDTH, :]
            else:
                dst[s, rows:rows + WIDTH, :] = src[1, low:low + WIDTH, :]

    load_force.wait()
    load_decay.wait()
    whole = slice(0, rows)
    for s in range(species):
        inverse = 1.0 / (1.0 + h * decay[s, whole, :])
        grow[s] = inverse
        shift[s] = h * force[s, whole, :] * inverse
        pack(side_send, 0, force, s)
        pack(side_send, WIDTH * species, decay, s)

    def present_count(flag):
        return flag.astype(jnp.int32)

    beside = present_count(has_left) + present_count(has_right)
    pl.semaphore_wait(barrier, beside + present_count(has_after) * (1 + beside))

    def pass_on(s):
        following[s] = grow[s] * start[s, whole, :] + shift[s]

        @pl.when(has_after)
        def _():
            start_copy(s).start()

        pack(edge_send, 0, following, s)

    def pass_edges():
        for k in range(2):
            @pl.when(has_after & sides[k][0])
            def _():
                edge_copy(k).start()

    @pl.when(n == 0)
    def _():
        load_start.wait()
        for s in range(species):
            pass_on(s)
        pass_edges()
        for s in range(species):
            pack(edge_first, 0, start, s)
        for k in range(2):
            @pl.when(sides[k][0])
            def _():
                first_copy(k).start()

    for k in range(2):
        @pl.when(sides[k][0])
        def _():
            side_copy(k).start()

    own_time = jnp.float32(0.0)
    own_row = [jnp.float32(0.0)] * nodes
    for i in range(nodes):
        own_time = jnp.where(m == i, jnp.float32(points[i]), own_time)
        own_row = [jnp.where(m == i, jnp.float32(table[i, j]), own_row[j]) for j in range(nodes)]
    own_stiff = own_time * jnp.float32(h / nodes)

    def prepare(s, part):
        d = decay[s, part, :]
        f = force[s, part, :]
        for j in range(nodes):
            inverse = 1.0 / (1.0 + float(points[j] * h) * d)
            node_inv[j, s, part, :] = inverse
            node_add[j, s, part, :] = float(points[j] * h) * f * inverse
            sweep_inv[j, s, part, :] = 1.0 / (1.0 + float(h * points[j] / nodes) * d)

    for s in range(species):
        prepare(s, whole)
        own_inv[s] = 1.0 / (1.0 + own_stiff * decay[s, whole, :])
    for k in range(2):
        @pl.when(sides[k][0])
        def _():
            side_copy(1 - k).wait_recv()
            unpack(force, side_recv, k, 0)
            unpack(decay, side_recv, k, WIDTH * species)
    for s in range(species):
        prepare(s, halo)

    def node_values(s, part):
        w = start[s, part, :]
        return [w * node_inv[j, s, part, :] + node_add[j, s, part, :] for j in range(nodes)]

    def interior_values(s):
        values = node_values(s, whole)
        for j in range(nodes):
            field[j, s, TILE:TILE + rows, :] = values[j]
            field[j, s, 2 * TILE + rows:3 * TILE + rows, :] = values[j][0:TILE]

    @pl.when(n == 0)
    def _():
        for s in range(species):
            interior_values(s)

    @pl.when(has_before)
    def _():
        for s in range(species):
            start_copy(s).wait_recv()
            pass_on(s)
            interior_values(s)
        pass_edges()

    for k in range(2):
        @pl.when(sides[k][0])
        def _():
            edge_copy(1 - k).wait_recv()
            unpack(start, edge_recv, k, 0)
    for s in range(species):
        values = node_values(s, halo)
        for j in range(nodes):
            field[j, s, 0:TILE, :] = values[j]
            field[j, s, TILE + rows:2 * TILE + rows, :] = values[j]

    for load in loads:
        load.wait()
    depth = lax.broadcasted_iota(jnp.int32, (TILE, cells), 1) % NZ
    is_first, is_last = depth == 0, depth == NZ - 1
    row = lax.broadcasted_iota(jnp.int32, (TILE, cells), 0)
    inside = ((row < WIDTH) & has_right) | ((row >= TILE - WIDTH) & has_left)

    def linear(ref, s, low, d):
        c = ref[s, low:low + TILE, :]
        x_plus = ref[s, low + 1:low + TILE + 1, :]
        x_minus = ref[s, low - 1:low + TILE - 1, :]
        y_plus = pltpu.roll(c, cells - NZ, 1)
        y_minus = pltpu.roll(c, NZ, 1)
        z_plus = jnp.where(is_last, 0.0, pltpu.roll(c, cells - 1, 1))
        z_minus = jnp.where(is_first, 0.0, pltpu.roll(c, 1, 1))
        dd = diff[s]
        vx, vy, vz = 0.5 * vel[0, s], 0.5 * vel[1, s], 0.5 * vel[2, s]
        return (
            ((dd - vx) * x_plus + (dd + vx) * x_minus)
            + ((dd - vy) * y_plus + (dd + vy) * y_minus)
            + ((dd - vz) * z_plus + (dd + vz) * z_minus)
            - (6.0 * dd + d) * c
        )

    def coupled(values, s):
        total = mix[s, 0] * values[0]
        for t in range(1, species):
            total = total + mix[s, t] * values[t]
        return jnp.tanh(total)

    for t in list(range(tiles)) + [tiles]:
        part = slice(TILE * t, TILE * t + TILE)
        low = TILE * (t + 1)
        is_halo = t == tiles
        fresh = [[None] * species for _ in range(nodes)]
        centers = [[field[j, s, low:low + TILE, :] for s in range(species)] for j in range(nodes)]
        for s in range(species):
            d = decay[s, part, :]
            f = force[s, part, :]
            w = start[s, part, :]
            rates = [linear(field.at[j], s, low, d) + coupled(centers[j], s) + f for j in range(nodes)]
            for i in range(nodes):
                total = float(h * table[i, 0]) * rates[0]
                for j in range(1, nodes):
                    total = total + float(h * table[i, j]) * rates[j]
                v = (w + total + float(h * points[i] / nodes) * d * centers[i][s]) * sweep_inv[i, s, part, :]
                fresh[i][s] = jnp.where(inside, v, 0.0) if is_halo else v
            if not is_halo:
                last_value[s, part, :] = fresh[nodes - 1][s]
            sum_now = own_row[0] * fresh[0][s]
            for j in range(1, nodes):
                sum_now = sum_now + own_row[j] * fresh[j][s]
            mixed[s, low:low + TILE, :] = sum_now
            if is_halo:
                mixed[s, 0:TILE, :] = sum_now
        if not is_halo:
            @pl.when(has_after)
            def _():
                hand_copy(t).start()

            for s in range(species):
                gained = own_time * force[s, part, :]
                own = fresh[0][s]
                for j in range(nodes):
                    gained = gained + own_row[j] * coupled(fresh[j], s)
                    if j > 0:
                        own = jnp.where(m == j, fresh[j][s], own)
                base[s, part, :] = h * gained + own_stiff * decay[s, part, :] * own

    for t in range(tiles):
        part = slice(TILE * t, TILE * t + TILE)
        for s in range(species):
            rate = linear(mixed, s, TILE * (t + 1), decay[s, part, :])
            base[s, part, :] = (base[s, part, :] + h * rate) * own_inv[s, part, :]

    @pl.when(n == 0)
    def _():
        load_handed.wait()

    for t in range(tiles):
        part = slice(TILE * t, TILE * t + TILE)

        @pl.when(has_before)
        def _():
            hand_copy(t).wait_recv()

        out_ref[0, 0, :, part, :] = handed[:, part, :] * own_inv[:, part, :] + base[:, part, :]

    for k in range(2):
        @pl.when(sides[k][0])
        def _():
            side_copy(k).wait_send()

        @pl.when(sides[k][0] & (n == 0))
        def _():
            first_copy(k).wait_send()

        @pl.when(sides[k][0] & has_after)
        def _():
            edge_copy(k).wait_send()

    @pl.when(has_after)
    def _():
        for s in range(species):
            start_copy(s).wait_send()
        for t in range(tiles):
            hand_copy(t).wait_send()


def body(*given):
    initial, _, _, mixing, diffusivity, velocity = given
    slices, pieces, nodes = (lax.axis_size(a) for a in ("tm", "space", "node"))
    species, rows, cells = initial.shape
    longer = rows + TILE
    packed = WIDTH * species
    tiles = rows // TILE
    f32 = jnp.float32
    dma = pltpu.SemaphoreType.DMA
    hbm = pl.BlockSpec(memory_space=pltpu.HBM)
    plain = pltpu.VMEM((species, rows, cells), f32)
    extended = pltpu.VMEM((species, longer, cells), f32)
    per_node = pltpu.VMEM((nodes, species, longer, cells), f32)
    return pl.pallas_call(
        functools.partial(kernel, slices, pieces, nodes),
        out_shape=jax.ShapeDtypeStruct((1, 1, species, rows, cells), f32),
        in_specs=[hbm] * 6,
        out_specs=pl.BlockSpec(memory_space=pltpu.VMEM),
        scratch_shapes=[
            pltpu.SMEM(mixing.shape, f32), pltpu.SMEM(diffusivity.shape, f32), pltpu.SMEM(velocity.shape, f32),
            extended, extended, extended, plain, plain, plain, plain,
            per_node, per_node, per_node, plain,
            pltpu.VMEM((nodes, species, rows + 3 * TILE, cells), f32),
            pltpu.VMEM((species, rows + 2 * TILE, cells), f32),
            plain, plain,
            pltpu.VMEM((2, 2 * packed, cells), f32),
            pltpu.VMEM((2, 2 * packed, cells), f32),
            pltpu.VMEM((2, packed, cells), f32),
            pltpu.VMEM((2, packed, cells), f32),
            pltpu.VMEM((2, packed, cells), f32),
            dma((7,)),
            dma((2,)), dma((2,)), dma((2,)), dma((2,)), dma((2,)),
            dma((species,)), dma((species,)), dma((tiles,)), dma((tiles,)),
        ],
        compiler_params=pltpu.CompilerParams(
            collective_id=0, has_side_effects=True, vmem_limit_bytes=24 * 1024 * 1024
        ),
    )(*(pltpu.with_memory_space_constraint(a, pltpu.HBM) for a in given))


def solution(mesh):
    placed = (
        P(None, "space", None),
        P("tm", None, "space", None),
        P(None, "space", None),
        P(),
        P(),
        P(),
    )
    return jax.shard_map(
        body,
        mesh=mesh,
        in_specs=placed,
        out_specs=P("tm", "node", None, "space", None),
        check_vma=False,
    )
```

```python
import functools

import jax
import jax.numpy as jnp
import numpy as np
from jax import lax
from jax.experimental import pallas as pl
from jax.experimental.pallas import tpu as pltpu
from jax.sharding import PartitionSpec as P

NZ = 16
WIDTH = 2
TILE = 8
LANES = 128

time_step = 0.05


def quadrature(node_count):
    points = [(position + 1.0) / node_count for position in range(node_count)]
    weights_table = np.zeros((node_count, node_count))
    for column in range(node_count):
        coeffs = [1.0]
        denominator = 1.0
        for other_node in range(node_count):
            if other_node != column:
                shifted = [0.0] + coeffs
                for degree in range(len(coeffs)):
                    shifted[degree] = shifted[degree] - points[other_node] * coeffs[degree]
                coeffs = shifted
                denominator = denominator * (points[column] - points[other_node])
        for row_node in range(node_count):
            running = 0.0
            for degree in range(len(coeffs)):
                running = running + coeffs[degree] * points[row_node] ** (degree + 1) / (degree + 1)
            weights_table[row_node, column] = running / denominator
    return (weights_table, np.array(points))


def kernel(
    slices, pieces, nodes,
    initial_hbm, forcing_hbm, decay_hbm, mix_hbm, diff_hbm, vel_hbm, out_ref,
    mix, diff, vel, start, force, decay, handed, following, grow, shift,
    coef, blend, diag, node_inv, node_add, sweep_inv, stiff, own_inv, own_stiff_inv,
    field, mixed, base, fresh,
    side_send, side_recv, edge_send, edge_first, edge_recv,
    load_sem,
    side_ss, side_rs, edge_ss, first_ss, edge_rs, start_ss, start_rs, hand_ss, hand_rs,
):
    species, rows, cells = following.shape
    tiles = rows // TILE
    halo = slice(rows, rows + TILE)
    h = time_step
    half = species // 2
    blocks = cells // LANES
    table, points = quadrature(nodes)
    n = lax.axis_index("tm")
    p = lax.axis_index("space")
    m = lax.axis_index("node")
    has_left, has_right = p > 0, p < pieces - 1
    has_before, has_after = n > 0, n < slices - 1
    sides = ((has_left, p - 1), (has_right, p + 1))
    mesh_id = pl.DeviceIdType.MESH

    barrier = pltpu.get_barrier_semaphore()

    def greet(condition, where):
        @pl.when(condition)
        def _():
            pl.semaphore_signal(barrier, inc=1, device_id=where, device_id_type=mesh_id)

    greet(has_before, {"tm": n - 1})
    for present, place in sides:
        greet(present, {"space": place})
        greet(present & has_before, {"tm": n - 1, "space": place})

    load_force = pltpu.make_async_copy(forcing_hbm.at[0], force.at[:, 0:rows], load_sem.at[0])
    load_decay = pltpu.make_async_copy(decay_hbm, decay.at[:, 0:rows], load_sem.at[1])
    load_start = pltpu.make_async_copy(initial_hbm, start.at[:, 0:rows], load_sem.at[2])
    load_handed = pltpu.make_async_copy(initial_hbm, handed, load_sem.at[3])
    loads = [
        pltpu.make_async_copy(src, dst, load_sem.at[4 + i])
        for i, (src, dst) in enumerate([(mix_hbm, mix), (diff_hbm, diff), (vel_hbm, vel)])
    ]
    load_force.start()
    load_decay.start()
    for load in loads:
        load.start()

    @pl.when(n == 0)
    def _():
        load_start.start()
        load_handed.start()

    zero_tile = jnp.zeros((species, TILE, cells), jnp.float32)
    start[:, halo, :] = zero_tile
    force[:, halo, :] = zero_tile
    decay[:, halo, :] = zero_tile

    def send(src, dst, ss, rs, where):
        return pltpu.make_async_remote_copy(
            src_ref=src, dst_ref=dst, send_sem=ss, recv_sem=rs, device_id=where, device_id_type=mesh_id
        )

    def side_copy(k):
        return send(side_send.at[k], side_recv.at[1 - k], side_ss.at[k], side_rs.at[1 - k], {"space": sides[k][1]})

    def first_copy(k):
        return send(edge_first.at[k], edge_recv.at[1 - k], first_ss.at[k], edge_rs.at[1 - k], {"space": sides[k][1]})

    def edge_copy(k):
        return send(
            edge_send.at[k], edge_recv.at[1 - k], edge_ss.at[k], edge_rs.at[1 - k],
            {"tm": n + 1, "space": sides[k][1]},
        )

    def start_copy(s):
        return send(following.at[s], start.at[s, 0:rows], start_ss.at[s], start_rs.at[s], {"tm": n + 1})

    def hand_copy(t, q):
        part = (pl.ds(q * half, half), pl.ds(TILE * t, TILE))
        return send(fresh.at[(nodes - 1,) + part], handed.at[part], hand_ss.at[t, q], hand_rs.at[t, q], {"tm": n + 1})

    def pack(dst, offset, src, s):
        low = offset + WIDTH * s
        dst[0, low:low + WIDTH, :] = src[s, 0:WIDTH, :]
        dst[1, low:low + WIDTH, :] = src[s, rows - WIDTH:rows, :]

    def unpack(dst, src, k, offset):
        for s in range(species):
            low = offset + WIDTH * s
            if k == 0:
                dst[s, rows + TILE - WIDTH:rows + TILE, :] = src[0, low:low + WIDTH, :]
            else:
                dst[s, rows:rows + WIDTH, :] = src[1, low:low + WIDTH, :]

    def present_count(flag):
        return flag.astype(jnp.int32)

    whole = slice(0, rows)

    def pass_on(s):
        following[s] = grow[s] * start[s, whole, :] + shift[s]

        @pl.when(has_after)
        def _():
            start_copy(s).start()

        pack(edge_send, 0, following, s)

    def pass_edges():
        for k in range(2):
            @pl.when(has_after & sides[k][0])
            def _():
                edge_copy(k).start()

    beside = present_count(has_left) + present_count(has_right)
    load_force.wait()
    load_decay.wait()

    @pl.when(n == 0)
    def _():
        load_start.wait()

    pl.semaphore_wait(barrier, beside + present_count(has_after) * (1 + beside))

    for s in range(species):
        inverse = 1.0 / (1.0 + h * decay[s, whole, :])
        grow[s] = inverse
        shift[s] = h * force[s, whole, :] * inverse

        @pl.when(n == 0)
        def _():
            pass_on(s)

    @pl.when(n == 0)
    def _():
        pass_edges()
        for s in range(species):
            pack(edge_first, 0, start, s)
        for k in range(2):
            @pl.when(sides[k][0])
            def _():
                first_copy(k).start()

    for s in range(species):
        pack(side_send, 0, force, s)
        pack(side_send, WIDTH * species, decay, s)
    for k in range(2):
        @pl.when(sides[k][0])
        def _():
            side_copy(k).start()

    own_time = jnp.float32(0.0)
    own_row = [jnp.float32(0.0)] * nodes
    for i in range(nodes):
        own_time = jnp.where(m == i, jnp.float32(points[i]), own_time)
        own_row = [jnp.where(m == i, jnp.float32(table[i, j]), own_row[j]) for j in range(nodes)]
    own_stiff = own_time * jnp.float32(h / nodes)

    for load in loads:
        load.wait()
    lane = lax.broadcasted_iota(jnp.int32, (TILE, LANES), 1)
    depth = lane % NZ
    is_first, is_last = depth == 0, depth == NZ - 1
    for s in range(species):
        dd = diff[s]
        drift = [0.5 * vel[i, s] for i in range(3)]
        for i in range(3):
            plus = jnp.full((TILE, LANES), dd - drift[i])
            minus = jnp.full((TILE, LANES), dd + drift[i])
            if i == 2:
                plus = jnp.where(is_last, 0.0, plus)
                minus = jnp.where(is_first, 0.0, minus)
            coef[s, 2 * i] = plus
            coef[s, 2 * i + 1] = minus
        for t in range(species):
            blend[s, t] = jnp.full((TILE, LANES), mix[s, t])

    def prepare(s, part):
        d = decay[s, part, :]
        f = force[s, part, :]
        diag[s, part, :] = d + 6.0 * diff[s]
        for j in range(nodes):
            inverse = 1.0 / (1.0 + float(points[j] * h) * d)
            node_inv[j, s, part, :] = inverse
            node_add[j, s, part, :] = float(points[j] * h) * f * inverse
            portion = float(h * points[j] / nodes) * d
            inverse = 1.0 / (1.0 + portion)
            sweep_inv[j, s, part, :] = inverse
            stiff[j, s, part, :] = portion * inverse

    for s in range(species):
        prepare(s, whole)
        portion = own_stiff * decay[s, whole, :]
        inverse = 1.0 / (1.0 + portion)
        own_inv[s] = inverse
        own_stiff_inv[s] = portion * inverse
    for k in range(2):
        @pl.when(sides[k][0])
        def _():
            side_copy(1 - k).wait_recv()
            unpack(force, side_recv, k, 0)
            unpack(decay, side_recv, k, WIDTH * species)
    for s in range(species):
        prepare(s, halo)

    def node_values(s, part):
        w = start[s, part, :]
        return [w * node_inv[j, s, part, :] + node_add[j, s, part, :] for j in range(nodes)]

    def interior_values(s):
        values = node_values(s, whole)
        for j in range(nodes):
            field[j, s, TILE:TILE + rows, :] = values[j]
            field[j, s, 2 * TILE + rows:3 * TILE + rows, :] = values[j][0:TILE]

    @pl.when(n == 0)
    def _():
        for s in range(species):
            interior_values(s)

    @pl.when(has_before)
    def _():
        for s in range(species):
            start_copy(s).wait_recv()
            pass_on(s)
            interior_values(s)
        pass_edges()

    for k in range(2):
        @pl.when(sides[k][0])
        def _():
            edge_copy(1 - k).wait_recv()
            unpack(start, edge_recv, k, 0)
    for s in range(species):
        values = node_values(s, halo)
        for j in range(nodes):
            field[j, s, 0:TILE, :] = values[j]
            field[j, s, TILE + rows:2 * TILE + rows, :] = values[j]

    row = lax.broadcasted_iota(jnp.int32, (TILE, LANES), 0)
    inside = ((row < WIDTH) & has_right) | ((row >= TILE - WIDTH) & has_left)
    y_up, y_down = lane < LANES - NZ, lane >= NZ
    block = [slice(LANES * b, LANES * (b + 1)) for b in range(blocks)]

    def pick(ref, s, part):
        return [ref[s, part, cut] for cut in block]

    def linear(ref, s, low, coefs, d):
        c = pick(ref, s, slice(low, low + TILE))
        x_plus = pick(ref, s, slice(low + 1, low + TILE + 1))
        x_minus = pick(ref, s, slice(low - 1, low + TILE - 1))
        up = [pltpu.roll(v, LANES - NZ, 1) for v in c]
        down = [pltpu.roll(v, NZ, 1) for v in c]
        total = []
        for b in range(blocks):
            y_plus = jnp.where(y_up, up[b], up[(b + 1) % blocks])
            y_minus = jnp.where(y_down, down[b], down[b - 1])
            total.append(
                (coefs[0] * x_plus[b] + coefs[1] * x_minus[b])
                + (coefs[2] * y_plus + coefs[3] * y_minus)
                + (coefs[4] * pltpu.roll(c[b], LANES - 1, 1) + coefs[5] * pltpu.roll(c[b], 1, 1))
                - d[b] * c[b]
            )
        return total

    def coupled(values, weights):
        result = []
        for b in range(blocks):
            total = weights[0] * values[0][b]
            for t in range(1, species):
                total = total + weights[t] * values[t][b]
            result.append(jnp.tanh(total))
        return result

    for t in range(tiles + 1):
        part = slice(TILE * t, TILE * t + TILE)
        low = TILE * (t + 1)
        is_halo = t == tiles
        centers = [[pick(field.at[j], s, slice(low, low + TILE)) for s in range(species)] for j in range(nodes)]
        for s in range(species):
            coefs = [coef[s, i] for i in range(6)]
            weights = [blend[s, i] for i in range(species)]
            d = pick(diag, s, part)
            f = pick(force, s, part)
            w = pick(start, s, part)
            rates = []
            for j in range(nodes):
                flow = linear(field.at[j], s, low, coefs, d)
                pull = coupled(centers[j], weights)
                rates.append([flow[b] + pull[b] + f[b] for b in range(blocks)])
            for b in range(blocks):
                sum_now = None
                for i in range(nodes):
                    total = w[b]
                    for j in range(nodes):
                        total = total + float(h * table[i, j]) * rates[j][b]
                    v = total * sweep_inv[i, s, part, block[b]] + centers[i][s][b] * stiff[i, s, part, block[b]]
                    if is_halo:
                        v = jnp.where(inside, v, 0.0)
                    else:
                        fresh[i, s, part, block[b]] = v
                    sum_now = own_row[i] * v if sum_now is None else sum_now + own_row[i] * v
                mixed[s, low:low + TILE, block[b]] = sum_now
                if is_halo:
                    mixed[s, 0:TILE, block[b]] = sum_now
            if not is_halo and (s + 1) % half == 0:
                @pl.when(has_after)
                def _():
                    hand_copy(t, s // half).start()

    for t in range(tiles):
        part = slice(TILE * t, TILE * t + TILE)
        centers = [[pick(fresh.at[j], s, part) for s in range(species)] for j in range(nodes)]
        for s in range(species):
            weights = [blend[s, i] for i in range(species)]
            coefs = [coef[s, i] for i in range(6)]
            flow = linear(mixed, s, TILE * (t + 1), coefs, pick(diag, s, part))
            pull = [coupled(centers[j], weights) for j in range(nodes)]
            f = pick(force, s, part)
            for b in range(blocks):
                total = flow[b] + own_time * f[b]
                own = centers[0][s][b]
                for j in range(nodes):
                    total = total + own_row[j] * pull[j][b]
                    if j > 0:
                        own = jnp.where(m == j, centers[j][s][b], own)
                base[s, part, block[b]] = h * total * own_inv[s, part, block[b]] + own * own_stiff_inv[s, part, block[b]]

    @pl.when(n == 0)
    def _():
        load_handed.wait()

    for t in range(tiles):
        part = slice(TILE * t, TILE * t + TILE)

        @pl.when(has_before)
        def _():
            for q in range(2):
                hand_copy(t, q).wait_recv()

        out_ref[0, 0, :, part, :] = handed[:, part, :] * own_inv[:, part, :] + base[:, part, :]

    for k in range(2):
        @pl.when(sides[k][0])
        def _():
            side_copy(k).wait_send()

        @pl.when(sides[k][0] & (n == 0))
        def _():
            first_copy(k).wait_send()

        @pl.when(sides[k][0] & has_after)
        def _():
            edge_copy(k).wait_send()

    @pl.when(has_after)
    def _():
        for s in range(species):
            start_copy(s).wait_send()
        for t in range(tiles):
            for q in range(2):
                hand_copy(t, q).wait_send()


def body(*given):
    initial, _, _, mixing, diffusivity, velocity = given
    slices, pieces, nodes = (lax.axis_size(a) for a in ("tm", "space", "node"))
    species, rows, cells = initial.shape
    longer = rows + TILE
    packed = WIDTH * species
    tiles = rows // TILE
    f32 = jnp.float32
    dma = pltpu.SemaphoreType.DMA
    hbm = pl.BlockSpec(memory_space=pltpu.HBM)
    plain = pltpu.VMEM((species, rows, cells), f32)
    extended = pltpu.VMEM((species, longer, cells), f32)
    per_node = pltpu.VMEM((nodes, species, longer, cells), f32)
    return pl.pallas_call(
        functools.partial(kernel, slices, pieces, nodes),
        out_shape=jax.ShapeDtypeStruct((1, 1, species, rows, cells), f32),
        in_specs=[hbm] * 6,
        out_specs=pl.BlockSpec(memory_space=pltpu.VMEM),
        scratch_shapes=[
            pltpu.SMEM(mixing.shape, f32), pltpu.SMEM(diffusivity.shape, f32), pltpu.SMEM(velocity.shape, f32),
            extended, extended, extended, plain, plain, plain, plain,
            pltpu.VMEM((species, 6, TILE, LANES), f32),
            pltpu.VMEM((species, species, TILE, LANES), f32),
            extended, per_node, per_node, per_node, per_node, plain, plain,
            pltpu.VMEM((nodes, species, rows + 3 * TILE, cells), f32),
            pltpu.VMEM((species, rows + 2 * TILE, cells), f32),
            plain, pltpu.VMEM((nodes, species, rows, cells), f32),
            pltpu.VMEM((2, 2 * packed, cells), f32),
            pltpu.VMEM((2, 2 * packed, cells), f32),
            pltpu.VMEM((2, packed, cells), f32),
            pltpu.VMEM((2, packed, cells), f32),
            pltpu.VMEM((2, packed, cells), f32),
            dma((7,)),
            dma((2,)), dma((2,)), dma((2,)), dma((2,)), dma((2,)),
            dma((species,)), dma((species,)), dma((tiles, 2)), dma((tiles, 2)),
        ],
        compiler_params=pltpu.CompilerParams(
            collective_id=0, has_side_effects=True, vmem_limit_bytes=24 * 1024 * 1024
        ),
    )(*(pltpu.with_memory_space_constraint(a, pltpu.HBM) for a in given))


def solution(mesh):
    placed = (
        P(None, "space", None),
        P("tm", None, "space", None),
        P(None, "space", None),
        P(),
        P(),
        P(),
    )
    return jax.shard_map(
        body,
        mesh=mesh,
        in_specs=placed,
        out_specs=P("tm", "node", None, "space", None),
        check_vma=False,
    )
```

```python
import functools

import jax
import jax.numpy as jnp
import numpy as np
from jax import lax
from jax.experimental import pallas as pl
from jax.experimental.pallas import tpu as pltpu
from jax.sharding import PartitionSpec as P

NZ = 16
WIDTH = 2
TILE = 8
GROUP = 2
LANES = 128

time_step = 0.05


def quadrature(node_count):
    points = [(position + 1.0) / node_count for position in range(node_count)]
    weights_table = np.zeros((node_count, node_count))
    for column in range(node_count):
        coeffs = [1.0]
        denominator = 1.0
        for other_node in range(node_count):
            if other_node != column:
                shifted = [0.0] + coeffs
                for degree in range(len(coeffs)):
                    shifted[degree] = shifted[degree] - points[other_node] * coeffs[degree]
                coeffs = shifted
                denominator = denominator * (points[column] - points[other_node])
        for row_node in range(node_count):
            running = 0.0
            for degree in range(len(coeffs)):
                running = running + coeffs[degree] * points[row_node] ** (degree + 1) / (degree + 1)
            weights_table[row_node, column] = running / denominator
    return (weights_table, np.array(points))


def kernel(
    slices, pieces, nodes,
    initial_hbm, forcing_hbm, decay_hbm, mix_hbm, diff_hbm, vel_hbm, out_ref,
    mix, diff, vel, start, force, decay, handed, following, grow, shift,
    coef, blend, diag, node_inv, node_add, sweep_inv, stiff, away, away_inv, pair_inv, pair_stiff,
    field, mixed, base, given, taken, fresh,
    side_send, side_recv, edge_send, edge_first, edge_recv,
    load_sem,
    side_ss, side_rs, edge_ss, first_ss, edge_rs, start_ss, start_rs, hand_ss, hand_rs, give_ss, give_rs,
):
    species, rows, cells = following.shape
    halo = slice(rows, rows + TILE)
    h = time_step
    half = species // 2
    blocks = cells // LANES
    table, points = quadrature(nodes)
    n = lax.axis_index("tm")
    p = lax.axis_index("space")
    m = lax.axis_index("node")
    part_now = lax.rem(m, 2)
    partner = m + 1 - 2 * part_now
    has_left, has_right = (p > 0) | (part_now == 1), (p < pieces - 1) | (part_now == 0)
    has_before, has_after = n > 0, n < slices - 1
    left = {"space": p - 1 + part_now, "node": partner}
    right = {"space": p + part_now, "node": partner}
    sides = ((has_left, left), (has_right, right))
    step = 2 * part_now - 1
    outer = {"space": p + step, "node": partner}
    present_outer = jnp.where(part_now == 1, p < pieces - 1, p > 0)
    here = pl.ds(pl.multiple_of(TILE * part_now, TILE), TILE)
    there = pl.ds(pl.multiple_of(TILE * (1 - part_now), TILE), TILE)
    mesh_id = pl.DeviceIdType.MESH

    barrier = pltpu.get_barrier_semaphore()

    def greet(condition, where):
        @pl.when(condition)
        def _():
            pl.semaphore_signal(barrier, inc=1, device_id=where, device_id_type=mesh_id)

    greet(m >= 0, {"node": partner})
    for where in ({"tm": n - 1}, {"tm": n - 1, "node": partner}):
        greet(has_before, where)
    greet(present_outer, outer)
    greet(present_outer & has_before, {"tm": n - 1, **outer})

    load_force = pltpu.make_async_copy(forcing_hbm.at[0, :, here], force.at[:, 0:rows], load_sem.at[0])
    load_decay = pltpu.make_async_copy(decay_hbm.at[:, here], decay.at[:, 0:rows], load_sem.at[1])
    load_start = pltpu.make_async_copy(initial_hbm.at[:, here], start.at[:, 0:rows], load_sem.at[2])
    load_handed = [
        pltpu.make_async_copy(initial_hbm.at[:, cut], handed.at[i], load_sem.at[7 + i])
        for i, cut in enumerate((here, there))
    ]
    load_away = pltpu.make_async_copy(decay_hbm.at[:, there], away, load_sem.at[3])
    loads = [
        pltpu.make_async_copy(src, dst, load_sem.at[4 + i])
        for i, (src, dst) in enumerate([(mix_hbm, mix), (diff_hbm, diff), (vel_hbm, vel)])
    ]
    load_force.start()
    load_decay.start()
    load_away.start()
    for load in loads:
        load.start()

    @pl.when(n == 0)
    def _():
        load_start.start()
        for load in load_handed:
            load.start()

    zero_tile = jnp.zeros((species, TILE, cells), jnp.float32)
    start[:, halo, :] = zero_tile
    force[:, halo, :] = zero_tile
    decay[:, halo, :] = zero_tile

    def send(src, dst, ss, rs, where):
        return pltpu.make_async_remote_copy(
            src_ref=src, dst_ref=dst, send_sem=ss, recv_sem=rs, device_id=where, device_id_type=mesh_id
        )

    def side_copy(k):
        return send(side_send.at[k], side_recv.at[1 - k], side_ss.at[k], side_rs.at[1 - k], sides[k][1])

    def first_copy(k):
        return send(edge_first.at[k], edge_recv.at[1 - k], first_ss.at[k], edge_rs.at[1 - k], sides[k][1])

    def edge_copy(k):
        return send(
            edge_send.at[k], edge_recv.at[1 - k], edge_ss.at[k], edge_rs.at[1 - k],
            {"tm": n + 1, **sides[k][1]},
        )

    def start_copy(c):
        group = pl.ds(GROUP * c, GROUP)
        return send(following.at[group], start.at[group, 0:rows], start_ss.at[c], start_rs.at[c], {"tm": n + 1})

    def hand_copy(i, q):
        group = pl.ds(q * half, half)
        where = {"tm": n + 1, "node": partner} if i else {"tm": n + 1}
        return send(fresh.at[nodes - 1, group], handed.at[i, group], hand_ss.at[i, q], hand_rs.at[i, q], where)

    def give_copy(q):
        group = pl.ds(q * half, half)
        return send(given.at[group], taken.at[group], give_ss.at[q], give_rs.at[q], {"node": partner})

    def pack(dst, offset, src, s):
        low = offset + WIDTH * s
        dst[0, low:low + WIDTH, :] = src[s, 0:WIDTH, :]
        dst[1, low:low + WIDTH, :] = src[s, rows - WIDTH:rows, :]

    def unpack(dst, src, k, offset):
        for s in range(species):
            low = offset + WIDTH * s
            if k == 0:
                dst[s, rows + TILE - WIDTH:rows + TILE, :] = src[0, low:low + WIDTH, :]
            else:
                dst[s, rows:rows + WIDTH, :] = src[1, low:low + WIDTH, :]

    def present_count(flag):
        return flag.astype(jnp.int32)

    whole = slice(0, rows)

    def pass_on(s):
        following[s] = grow[s] * start[s, whole, :] + shift[s]

        if (s + 1) % GROUP == 0:
            @pl.when(has_after)
            def _():
                start_copy(s // GROUP).start()

        pack(edge_send, 0, following, s)

    def pass_edges():
        for k in range(2):
            @pl.when(has_after & sides[k][0])
            def _():
                edge_copy(k).start()

    beside = 1 + present_count(present_outer)
    load_force.wait()
    load_decay.wait()

    @pl.when(n == 0)
    def _():
        load_start.wait()

    pl.semaphore_wait(barrier, beside + present_count(has_after) * (1 + beside))

    for s in range(species):
        inverse = 1.0 / (1.0 + h * decay[s, whole, :])
        grow[s] = inverse
        shift[s] = h * force[s, whole, :] * inverse

        @pl.when(n == 0)
        def _():
            pass_on(s)

    @pl.when(n == 0)
    def _():
        pass_edges()
        for s in range(species):
            pack(edge_first, 0, start, s)
        for k in range(2):
            @pl.when(sides[k][0])
            def _():
                first_copy(k).start()

    for s in range(species):
        pack(side_send, 0, force, s)
        pack(side_send, WIDTH * species, decay, s)
    for k in range(2):
        @pl.when(sides[k][0])
        def _():
            side_copy(k).start()

    def node_scalars(which):
        time, weights = jnp.float32(0.0), [jnp.float32(0.0)] * nodes
        for i in range(nodes):
            time = jnp.where(which == i, jnp.float32(points[i]), time)
            weights = [jnp.where(which == i, jnp.float32(table[i, j]), weights[j]) for j in range(nodes)]
        return time, weights, time * jnp.float32(h / nodes)

    pair = [(m,) + node_scalars(m), (partner,) + node_scalars(partner)]

    for load in loads:
        load.wait()
    lane = lax.broadcasted_iota(jnp.int32, (TILE, LANES), 1)
    depth = lane % NZ
    is_first, is_last = depth == 0, depth == NZ - 1
    for s in range(species):
        dd = diff[s]
        drift = [0.5 * vel[i, s] for i in range(3)]
        for i in range(3):
            plus = jnp.full((TILE, LANES), dd - drift[i])
            minus = jnp.full((TILE, LANES), dd + drift[i])
            if i == 2:
                plus = jnp.where(is_last, 0.0, plus)
                minus = jnp.where(is_first, 0.0, minus)
            coef[s, 2 * i] = plus
            coef[s, 2 * i + 1] = minus
        for t in range(species):
            blend[s, t] = jnp.full((TILE, LANES), mix[s, t])

    def prepare(s, part):
        d = decay[s, part, :]
        f = force[s, part, :]
        diag[s, part, :] = d + 6.0 * diff[s]
        for j in range(nodes):
            inverse = 1.0 / (1.0 + float(points[j] * h) * d)
            node_inv[j, s, part, :] = inverse
            node_add[j, s, part, :] = float(points[j] * h) * f * inverse
            portion = float(h * points[j] / nodes) * d
            inverse = 1.0 / (1.0 + portion)
            sweep_inv[j, s, part, :] = inverse
            stiff[j, s, part, :] = portion * inverse

    for s in range(species):
        prepare(s, whole)
        for i in range(2):
            portion = pair[i][3] * decay[s, whole, :]
            inverse = 1.0 / (1.0 + portion)
            pair_inv[i, s] = inverse
            pair_stiff[i, s] = portion * inverse
    load_away.wait()
    for s in range(species):
        away_inv[s] = 1.0 / (1.0 + pair[0][3] * away[s])
    for k in range(2):
        @pl.when(sides[k][0])
        def _():
            side_copy(1 - k).wait_recv()
            unpack(force, side_recv, k, 0)
            unpack(decay, side_recv, k, WIDTH * species)
    for s in range(species):
        prepare(s, halo)

    def node_values(s, part):
        w = start[s, part, :]
        return [w * node_inv[j, s, part, :] + node_add[j, s, part, :] for j in range(nodes)]

    def interior_values(s):
        values = node_values(s, whole)
        for j in range(nodes):
            field[j, s, TILE:TILE + rows, :] = values[j]
            field[j, s, 2 * TILE + rows:3 * TILE + rows, :] = values[j][0:TILE]

    @pl.when(n == 0)
    def _():
        for s in range(species):
            interior_values(s)

    @pl.when(has_before)
    def _():
        for s in range(species):
            if s % GROUP == 0:
                start_copy(s // GROUP).wait_recv()
            pass_on(s)
            interior_values(s)
        pass_edges()

    for k in range(2):
        @pl.when(sides[k][0])
        def _():
            edge_copy(1 - k).wait_recv()
            unpack(start, edge_recv, k, 0)
    for s in range(species):
        values = node_values(s, halo)
        for j in range(nodes):
            field[j, s, 0:TILE, :] = values[j]
            field[j, s, TILE + rows:2 * TILE + rows, :] = values[j]

    row = lax.broadcasted_iota(jnp.int32, (TILE, LANES), 0)
    inside = ((row < WIDTH) & has_right) | ((row >= TILE - WIDTH) & has_left)
    y_up, y_down = lane < LANES - NZ, lane >= NZ
    block = [slice(LANES * b, LANES * (b + 1)) for b in range(blocks)]

    def pick(ref, s, part):
        return [ref[s, part, cut] for cut in block]

    def linear(ref, s, low, coefs, d):
        c = pick(ref, s, slice(low, low + TILE))
        x_plus = pick(ref, s, slice(low + 1, low + TILE + 1))
        x_minus = pick(ref, s, slice(low - 1, low + TILE - 1))
        up = [pltpu.roll(v, LANES - NZ, 1) for v in c]
        down = [pltpu.roll(v, NZ, 1) for v in c]
        total = []
        for b in range(blocks):
            y_plus = jnp.where(y_up, up[b], up[(b + 1) % blocks])
            y_minus = jnp.where(y_down, down[b], down[b - 1])
            total.append(
                (coefs[0] * x_plus[b] + coefs[1] * x_minus[b])
                + (coefs[2] * y_plus + coefs[3] * y_minus)
                + (coefs[4] * pltpu.roll(c[b], LANES - 1, 1) + coefs[5] * pltpu.roll(c[b], 1, 1))
                - d[b] * c[b]
            )
        return total

    def coupled(values, weights):
        result = []
        for b in range(blocks):
            total = weights[0] * values[0][b]
            for t in range(1, species):
                total = total + weights[t] * values[t][b]
            result.append(jnp.tanh(total))
        return result

    for t in range(2):
        part = slice(TILE * t, TILE * t + TILE)
        low = TILE * (t + 1)
        is_halo = t == 1
        centers = [[pick(field.at[j], s, slice(low, low + TILE)) for s in range(species)] for j in range(nodes)]
        for s in range(species):
            coefs = [coef[s, i] for i in range(6)]
            weights = [blend[s, i] for i in range(species)]
            d = pick(diag, s, part)
            f = pick(force, s, part)
            w = pick(start, s, part)
            rates = []
            for j in range(nodes):
                flow = linear(field.at[j], s, low, coefs, d)
                pull = coupled(centers[j], weights)
                rates.append([flow[b] + pull[b] + f[b] for b in range(blocks)])
            for b in range(blocks):
                sums = [0.0, 0.0]
                for i in range(nodes):
                    total = w[b]
                    for j in range(nodes):
                        total = total + float(h * table[i, j]) * rates[j][b]
                    v = total * sweep_inv[i, s, part, block[b]] + centers[i][s][b] * stiff[i, s, part, block[b]]
                    if is_halo:
                        v = jnp.where(inside, v, 0.0)
                    else:
                        fresh[i, s, part, block[b]] = v
                    sums = [sums[e] + pair[e][2][i] * v for e in range(2)]
                for e in range(2):
                    mixed[e, s, low:low + TILE, block[b]] = sums[e]
                    if is_halo:
                        mixed[e, s, 0:TILE, block[b]] = sums[e]
            if not is_halo and (s + 1) % half == 0:
                @pl.when(has_after)
                def _():
                    for i in range(2):
                        hand_copy(i, s // half).start()

    centers = [[pick(fresh.at[j], s, whole) for s in range(species)] for j in range(nodes)]
    for s in range(species):
        weights = [blend[s, i] for i in range(species)]
        coefs = [coef[s, i] for i in range(6)]
        d = pick(diag, s, whole)
        f = pick(force, s, whole)
        pull = [coupled(centers[j], weights) for j in range(nodes)]
        for e in (1, 0):
            which, time, row_weights, _ = pair[e]
            flow = linear(mixed.at[e], s, TILE, coefs, d)
            for b in range(blocks):
                total = flow[b] + time * f[b]
                own = centers[0][s][b]
                for j in range(nodes):
                    total = total + row_weights[j] * pull[j][b]
                    if j > 0:
                        own = jnp.where(which == j, centers[j][s][b], own)
                value = h * total * pair_inv[e, s, :, block[b]] + own * pair_stiff[e, s, :, block[b]]
                if e:
                    given[s, :, block[b]] = value
                else:
                    base[s, :, block[b]] = value
        if (s + 1) % half == 0:
            give_copy(s // half).start()

    @pl.when(n == 0)
    def _():
        for load in load_handed:
            load.wait()

    for q in range(2):
        group = slice(q * half, (q + 1) * half)

        @pl.when(has_before)
        def _():
            hand_copy(0, q).wait_recv()

        out_ref[0, 0, group, here, :] = handed[0, group] * pair_inv[0, group] + base[group]
    for q in range(2):
        group = slice(q * half, (q + 1) * half)

        @pl.when(has_before)
        def _():
            hand_copy(1, q).wait_recv()

        give_copy(q).wait_recv()
        out_ref[0, 0, group, there, :] = handed[1, group] * away_inv[group] + taken[group]

    for q in range(2):
        give_copy(q).wait_send()
    for k in range(2):
        @pl.when(sides[k][0])
        def _():
            side_copy(k).wait_send()

        @pl.when(sides[k][0] & (n == 0))
        def _():
            first_copy(k).wait_send()

        @pl.when(sides[k][0] & has_after)
        def _():
            edge_copy(k).wait_send()

    @pl.when(has_after)
    def _():
        for c in range(species // GROUP):
            start_copy(c).wait_send()
        for i in range(2):
            for q in range(2):
                hand_copy(i, q).wait_send()


def body(*given):
    initial, _, _, mixing, diffusivity, velocity = given
    slices, pieces, nodes = (lax.axis_size(a) for a in ("tm", "space", "node"))
    species, rows, cells = initial.shape
    assert rows == 2 * TILE and nodes % 2 == 0
    longer = 2 * TILE
    packed = WIDTH * species
    groups = species // GROUP
    f32 = jnp.float32
    dma = pltpu.SemaphoreType.DMA
    hbm = pl.BlockSpec(memory_space=pltpu.HBM)
    plain = pltpu.VMEM((species, TILE, cells), f32)
    twice = pltpu.VMEM((2, species, TILE, cells), f32)
    extended = pltpu.VMEM((species, longer, cells), f32)
    per_node = pltpu.VMEM((nodes, species, longer, cells), f32)
    return pl.pallas_call(
        functools.partial(kernel, slices, pieces, nodes),
        out_shape=jax.ShapeDtypeStruct((1, 1, species, rows, cells), f32),
        in_specs=[hbm] * 6,
        out_specs=pl.BlockSpec(memory_space=pltpu.VMEM),
        scratch_shapes=[
            pltpu.SMEM(mixing.shape, f32), pltpu.SMEM(diffusivity.shape, f32), pltpu.SMEM(velocity.shape, f32),
            extended, extended, extended, twice, plain, plain, plain,
            pltpu.VMEM((species, 6, TILE, LANES), f32),
            pltpu.VMEM((species, species, TILE, LANES), f32),
            extended, per_node, per_node, per_node, per_node, plain, plain, twice, twice,
            pltpu.VMEM((nodes, species, 4 * TILE, cells), f32),
            pltpu.VMEM((2, species, 3 * TILE, cells), f32),
            plain, plain, plain, pltpu.VMEM((nodes, species, TILE, cells), f32),
            pltpu.VMEM((2, 2 * packed, cells), f32),
            pltpu.VMEM((2, 2 * packed, cells), f32),
            pltpu.VMEM((2, packed, cells), f32),
            pltpu.VMEM((2, packed, cells), f32),
            pltpu.VMEM((2, packed, cells), f32),
            dma((9,)),
            dma((2,)), dma((2,)), dma((2,)), dma((2,)), dma((2,)),
            dma((groups,)), dma((groups,)), dma((2, 2)), dma((2, 2)), dma((2,)), dma((2,)),
        ],
        compiler_params=pltpu.CompilerParams(
            collective_id=0, has_side_effects=True, vmem_limit_bytes=24 * 1024 * 1024
        ),
    )(*(pltpu.with_memory_space_constraint(a, pltpu.HBM) for a in given))


def solution(mesh):
    placed = (
        P(None, "space", None),
        P("tm", None, "space", None),
        P(None, "space", None),
        P(),
        P(),
        P(),
    )
    return jax.shard_map(
        body,
        mesh=mesh,
        in_specs=placed,
        out_specs=P("tm", "node", None, "space", None),
        check_vma=False,
    )
```

```python
import functools

import jax
import jax.numpy as jnp
import numpy as np
from jax import lax
from jax.experimental import pallas as pl
from jax.experimental.pallas import tpu as pltpu
from jax.sharding import PartitionSpec as P

NZ = 16
WIDTH = 2
TILE = 8

time_step = 0.05


def quadrature(node_count):
    points = [(position + 1.0) / node_count for position in range(node_count)]
    weights_table = np.zeros((node_count, node_count))
    for column in range(node_count):
        coeffs = [1.0]
        denominator = 1.0
        for other_node in range(node_count):
            if other_node != column:
                shifted = [0.0] + coeffs
                for degree in range(len(coeffs)):
                    shifted[degree] = shifted[degree] - points[other_node] * coeffs[degree]
                coeffs = shifted
                denominator = denominator * (points[column] - points[other_node])
        for row_node in range(node_count):
            running = 0.0
            for degree in range(len(coeffs)):
                running = running + coeffs[degree] * points[row_node] ** (degree + 1) / (degree + 1)
            weights_table[row_node, column] = running / denominator
    return (weights_table, np.array(points))


def kernel(
    slices, pieces, nodes,
    initial_hbm, forcing_hbm, decay_hbm, mix_hbm, diff_hbm, vel_hbm, out_ref,
    mix, diff, vel, incoming, earlier, earlier_halo, start, force, decay, handed, following, grow, shift,
    node_inv, node_add, sweep_inv, own_inv,
    field, mixed, base, last_value,
    side_send, side_recv, edge_send, edge_first, edge_recv,
    early_recv, load_sem,
    side_ss, side_rs, edge_ss, first_ss, edge_rs, start_ss, start_rs, hand_ss, hand_rs, early_ss, early_rs, rim_ss, rim_rs,
):
    species, rows, cells = following.shape
    tiles = rows // TILE
    halo = slice(rows, rows + TILE)
    h = time_step
    table, points = quadrature(nodes)
    n = lax.axis_index("tm")
    p = lax.axis_index("space")
    m = lax.axis_index("node")
    has_left, has_right = p > 0, p < pieces - 1
    has_before, has_after = n > 0, n < slices - 1
    is_even = lax.rem(n, 2) == 0
    is_odd = lax.rem(n, 2) == 1
    far_before, far_after = is_even & (n > 1), is_even & (n < slices - 2)
    part_now = lax.rem(m, 2)
    partner = m + 1 - 2 * part_now
    half = species // 2
    own_half = pl.ds(part_now * half, half)
    other_half = pl.ds((1 - part_now) * half, half)
    sides = ((has_left, p - 1), (has_right, p + 1))
    mesh_id = pl.DeviceIdType.MESH

    barrier = pltpu.get_barrier_semaphore()

    def greet(condition, where):
        @pl.when(condition)
        def _():
            pl.semaphore_signal(barrier, inc=1, device_id=where, device_id_type=mesh_id)

    greet(has_before, {"tm": n - 1})
    for present, place in sides:
        greet(present, {"space": place})
        greet(present & has_before, {"tm": n - 1, "space": place})
        greet(present & far_before, {"tm": n - 2, "space": place})
    greet(far_before, {"tm": n - 2})
    greet(far_before, {"node": partner})

    load_force = pltpu.make_async_copy(forcing_hbm.at[0], force.at[:, 0:rows], load_sem.at[0])
    load_decay = pltpu.make_async_copy(decay_hbm, decay.at[:, 0:rows], load_sem.at[1])
    load_start = pltpu.make_async_copy(initial_hbm, start.at[:, 0:rows], load_sem.at[2])
    load_handed = pltpu.make_async_copy(initial_hbm, handed, load_sem.at[3])
    loads = [
        pltpu.make_async_copy(src, dst, load_sem.at[4 + i])
        for i, (src, dst) in enumerate([(mix_hbm, mix), (diff_hbm, diff), (vel_hbm, vel)])
    ]
    load_force.start()
    load_decay.start()
    for load in loads:
        load.start()

    @pl.when(n == 0)
    def _():
        load_start.start()
        load_handed.start()

    zero_tile = jnp.zeros((species, TILE, cells), jnp.float32)
    start[:, halo, :] = zero_tile
    force[:, halo, :] = zero_tile
    earlier_halo[...] = zero_tile
    decay[:, halo, :] = zero_tile

    def send(src, dst, ss, rs, where):
        return pltpu.make_async_remote_copy(
            src_ref=src, dst_ref=dst, send_sem=ss, recv_sem=rs, device_id=where, device_id_type=mesh_id
        )

    def side_copy(k):
        return send(side_send.at[k], side_recv.at[1 - k], side_ss.at[k], side_rs.at[1 - k], {"space": sides[k][1]})

    def first_copy(k):
        return send(edge_first.at[k], edge_recv.at[1 - k], first_ss.at[k], edge_rs.at[1 - k], {"space": sides[k][1]})

    def edge_copy(k, ahead):
        return send(
            edge_send.at[k], edge_recv.at[1 - k], edge_ss.at[ahead - 1, k], edge_rs.at[1 - k],
            {"tm": n + ahead, "space": sides[k][1]},
        )

    def start_copy(s, ahead):
        return send(following.at[s], incoming.at[s], start_ss.at[ahead - 1, s], start_rs.at[s], {"tm": n + ahead})

    def early_copy():
        return send(
            force.at[own_half, 0:rows], earlier.at[own_half], early_ss.at[0], early_rs.at[0], {"tm": n + 1}
        )

    def swap_copy():
        return send(earlier.at[own_half], earlier.at[own_half], early_ss.at[1], early_rs.at[1], {"node": partner})

    def swap_arrival():
        return send(earlier.at[other_half], earlier.at[other_half], early_ss.at[1], early_rs.at[1], {"node": partner})

    def rim_copy(k):
        return send(
            side_send.at[k, 0:WIDTH * species], early_recv.at[1 - k], rim_ss.at[k], rim_rs.at[1 - k],
            {"tm": n + 1, "space": sides[k][1]},
        )

    def hand_copy(t):
        part = pl.ds(TILE * t, TILE)
        return send(last_value.at[:, part], handed.at[:, part], hand_ss.at[t], hand_rs.at[t], {"tm": n + 1})

    def pack(dst, offset, src, s):
        low = offset + WIDTH * s
        dst[0, low:low + WIDTH, :] = src[s, 0:WIDTH, :]
        dst[1, low:low + WIDTH, :] = src[s, rows - WIDTH:rows, :]

    def unpack(dst, src, k, offset):
        for s in range(species):
            low = offset + WIDTH * s
            if k == 0:
                dst[s, rows + TILE - WIDTH:rows + TILE, :] = src[0, low:low + WIDTH, :]
            else:
                dst[s, rows:rows + WIDTH, :] = src[1, low:low + WIDTH, :]

    load_force.wait()
    load_decay.wait()
    whole = slice(0, rows)
    for s in range(species):
        inverse = 1.0 / (1.0 + h * decay[s, whole, :])
        grow[s] = inverse
        shift[s] = h * force[s, whole, :] * inverse
        pack(side_send, 0, force, s)
        pack(side_send, WIDTH * species, decay, s)

    def present_count(flag):
        return flag.astype(jnp.int32)

    beside = present_count(has_left) + present_count(has_right)
    pl.semaphore_wait(
        barrier,
        beside + (present_count(has_after) + present_count(far_after)) * (1 + beside) + present_count(far_before),
    )

    @pl.when(is_odd & has_after)
    def _():
        early_copy().start()
        for k in range(2):
            @pl.when(sides[k][0])
            def _():
                rim_copy(k).start()

    def pass_on(s):
        following[s] = grow[s] * start[s, whole, :] + shift[s]
        for ahead, present in ((2, far_after), (1, has_after)):
            @pl.when(present)
            def _():
                start_copy(s, ahead).start()

        pack(edge_send, 0, following, s)

    def pass_edges():
        for ahead, present in ((2, far_after), (1, has_after)):
            for k in range(2):
                @pl.when(present & sides[k][0])
                def _():
                    edge_copy(k, ahead).start()

    @pl.when(n == 0)
    def _():
        load_start.wait()
        for s in range(species):
            pass_on(s)
        pass_edges()
        for s in range(species):
            pack(edge_first, 0, start, s)
        for k in range(2):
            @pl.when(sides[k][0])
            def _():
                first_copy(k).start()

    for k in range(2):
        @pl.when(sides[k][0])
        def _():
            side_copy(k).start()

    own_time = jnp.float32(0.0)
    own_row = [jnp.float32(0.0)] * nodes
    for i in range(nodes):
        own_time = jnp.where(m == i, jnp.float32(points[i]), own_time)
        own_row = [jnp.where(m == i, jnp.float32(table[i, j]), own_row[j]) for j in range(nodes)]
    own_stiff = own_time * jnp.float32(h / nodes)

    def prepare(s, part):
        d = decay[s, part, :]
        f = force[s, part, :]
        for j in range(nodes):
            inverse = 1.0 / (1.0 + float(points[j] * h) * d)
            node_inv[j, s, part, :] = inverse
            node_add[j, s, part, :] = float(points[j] * h) * f * inverse
            sweep_inv[j, s, part, :] = 1.0 / (1.0 + float(h * points[j] / nodes) * d)

    for s in range(species):
        prepare(s, whole)
        own_inv[s] = 1.0 / (1.0 + own_stiff * decay[s, whole, :])
    for k in range(2):
        @pl.when(sides[k][0])
        def _():
            side_copy(1 - k).wait_recv()
            unpack(force, side_recv, k, 0)
            unpack(decay, side_recv, k, WIDTH * species)
    for s in range(species):
        prepare(s, halo)

    def node_values(s, part):
        w = start[s, part, :]
        return [w * node_inv[j, s, part, :] + node_add[j, s, part, :] for j in range(nodes)]

    def interior_values(s):
        values = node_values(s, whole)
        for j in range(nodes):
            field[j, s, TILE:TILE + rows, :] = values[j]
            field[j, s, 2 * TILE + rows:3 * TILE + rows, :] = values[j][0:TILE]

    @pl.when(n == 0)
    def _():
        for s in range(species):
            interior_values(s)

    @pl.when(is_odd)
    def _():
        for s in range(species):
            start_copy(s, 1).wait_recv()
            start[s, whole, :] = incoming[s]
            interior_values(s)

    @pl.when(far_before)
    def _():
        early_copy().wait_recv()
        swap_copy().start()
        for k in range(2):
            @pl.when(sides[k][0])
            def _():
                rim_copy(1 - k).wait_recv()
                for s in range(species):
                    low = WIDTH * s
                    if k == 0:
                        earlier_halo[s, TILE - WIDTH:TILE, :] = early_recv[0, low:low + WIDTH, :]
                    else:
                        earlier_halo[s, 0:WIDTH, :] = early_recv[1, low:low + WIDTH, :]
        swap_arrival().wait_recv()
        swap_copy().wait_send()
        for s in range(species):
            earlier[s] = h * earlier[s] * grow[s]
        for s in range(species):
            start_copy(s, 2).wait_recv()
            start[s, whole, :] = grow[s] * incoming[s] + earlier[s]
            pass_on(s)
            interior_values(s)
        pass_edges()

    for k in range(2):
        @pl.when(sides[k][0])
        def _():
            edge_copy(1 - k, 1).wait_recv()
            unpack(start, edge_recv, k, 0)

    @pl.when(far_before)
    def _():
        for s in range(species):
            inverse = 1.0 / (1.0 + h * decay[s, halo, :])
            start[s, halo, :] = (start[s, halo, :] + h * earlier_halo[s]) * inverse

    for s in range(species):
        values = node_values(s, halo)
        for j in range(nodes):
            field[j, s, 0:TILE, :] = values[j]
            field[j, s, TILE + rows:2 * TILE + rows, :] = values[j]

    for load in loads:
        load.wait()
    depth = lax.broadcasted_iota(jnp.int32, (TILE, cells), 1) % NZ
    is_first, is_last = depth == 0, depth == NZ - 1
    row = lax.broadcasted_iota(jnp.int32, (TILE, cells), 0)
    inside = ((row < WIDTH) & has_right) | ((row >= TILE - WIDTH) & has_left)

    def linear(ref, s, low, d):
        c = ref[s, low:low + TILE, :]
        x_plus = ref[s, low + 1:low + TILE + 1, :]
        x_minus = ref[s, low - 1:low + TILE - 1, :]
        y_plus = pltpu.roll(c, cells - NZ, 1)
        y_minus = pltpu.roll(c, NZ, 1)
        z_plus = jnp.where(is_last, 0.0, pltpu.roll(c, cells - 1, 1))
        z_minus = jnp.where(is_first, 0.0, pltpu.roll(c, 1, 1))
        dd = diff[s]
        vx, vy, vz = 0.5 * vel[0, s], 0.5 * vel[1, s], 0.5 * vel[2, s]
        return (
            ((dd - vx) * x_plus + (dd + vx) * x_minus)
            + ((dd - vy) * y_plus + (dd + vy) * y_minus)
            + ((dd - vz) * z_plus + (dd + vz) * z_minus)
            - (6.0 * dd + d) * c
        )

    def coupled(values, s):
        total = mix[s, 0] * values[0]
        for t in range(1, species):
            total = total + mix[s, t] * values[t]
        return jnp.tanh(total)

    for t in list(range(tiles)) + [tiles]:
        part = slice(TILE * t, TILE * t + TILE)
        low = TILE * (t + 1)
        is_halo = t == tiles
        fresh = [[None] * species for _ in range(nodes)]
        centers = [[field[j, s, low:low + TILE, :] for s in range(species)] for j in range(nodes)]
        for s in range(species):
            d = decay[s, part, :]
            f = force[s, part, :]
            w = start[s, part, :]
            rates = [linear(field.at[j], s, low, d) + coupled(centers[j], s) + f for j in range(nodes)]
            for i in range(nodes):
                total = float(h * table[i, 0]) * rates[0]
                for j in range(1, nodes):
                    total = total + float(h * table[i, j]) * rates[j]
                v = (w + total + float(h * points[i] / nodes) * d * centers[i][s]) * sweep_inv[i, s, part, :]
                fresh[i][s] = jnp.where(inside, v, 0.0) if is_halo else v
            if not is_halo:
                last_value[s, part, :] = fresh[nodes - 1][s]
            sum_now = own_row[0] * fresh[0][s]
            for j in range(1, nodes):
                sum_now = sum_now + own_row[j] * fresh[j][s]
            mixed[s, low:low + TILE, :] = sum_now
            if is_halo:
                mixed[s, 0:TILE, :] = sum_now
        if not is_halo:
            @pl.when(has_after)
            def _():
                hand_copy(t).start()

            for s in range(species):
                gained = own_time * force[s, part, :]
                own = fresh[0][s]
                for j in range(nodes):
                    gained = gained + own_row[j] * coupled(fresh[j], s)
                    if j > 0:
                        own = jnp.where(m == j, fresh[j][s], own)
                base[s, part, :] = h * gained + own_stiff * decay[s, part, :] * own

    for t in range(tiles):
        part = slice(TILE * t, TILE * t + TILE)
        for s in range(species):
            rate = linear(mixed, s, TILE * (t + 1), decay[s, part, :])
            base[s, part, :] = (base[s, part, :] + h * rate) * own_inv[s, part, :]

    @pl.when(n == 0)
    def _():
        load_handed.wait()

    for t in range(tiles):
        part = slice(TILE * t, TILE * t + TILE)

        @pl.when(has_before)
        def _():
            hand_copy(t).wait_recv()

        out_ref[0, 0, :, part, :] = handed[:, part, :] * own_inv[:, part, :] + base[:, part, :]

    for k in range(2):
        @pl.when(sides[k][0])
        def _():
            side_copy(k).wait_send()

        @pl.when(sides[k][0] & (n == 0))
        def _():
            first_copy(k).wait_send()

        for ahead, present in ((2, far_after), (1, has_after & is_even)):
            @pl.when(sides[k][0] & present)
            def _():
                edge_copy(k, ahead).wait_send()

        @pl.when(sides[k][0] & has_after & is_odd)
        def _():
            rim_copy(k).wait_send()

    @pl.when(has_after)
    def _():
        for t in range(tiles):
            hand_copy(t).wait_send()

    for ahead, present in ((2, far_after), (1, has_after & is_even)):
        @pl.when(present)
        def _():
            for s in range(species):
                start_copy(s, ahead).wait_send()

    @pl.when(has_after & is_odd)
    def _():
        early_copy().wait_send()


def body(*given):
    initial, _, _, mixing, diffusivity, velocity = given
    slices, pieces, nodes = (lax.axis_size(a) for a in ("tm", "space", "node"))
    species, rows, cells = initial.shape
    longer = rows + TILE
    packed = WIDTH * species
    tiles = rows // TILE
    f32 = jnp.float32
    dma = pltpu.SemaphoreType.DMA
    hbm = pl.BlockSpec(memory_space=pltpu.HBM)
    plain = pltpu.VMEM((species, rows, cells), f32)
    extended = pltpu.VMEM((species, longer, cells), f32)
    per_node = pltpu.VMEM((nodes, species, longer, cells), f32)
    return pl.pallas_call(
        functools.partial(kernel, slices, pieces, nodes),
        out_shape=jax.ShapeDtypeStruct((1, 1, species, rows, cells), f32),
        in_specs=[hbm] * 6,
        out_specs=pl.BlockSpec(memory_space=pltpu.VMEM),
        scratch_shapes=[
            pltpu.SMEM(mixing.shape, f32), pltpu.SMEM(diffusivity.shape, f32), pltpu.SMEM(velocity.shape, f32),
            plain, plain, pltpu.VMEM((species, TILE, cells), f32),
            extended, extended, extended, plain, plain, plain, plain,
            per_node, per_node, per_node, plain,
            pltpu.VMEM((nodes, species, rows + 3 * TILE, cells), f32),
            pltpu.VMEM((species, rows + 2 * TILE, cells), f32),
            plain, plain,
            pltpu.VMEM((2, 2 * packed, cells), f32),
            pltpu.VMEM((2, 2 * packed, cells), f32),
            pltpu.VMEM((2, packed, cells), f32),
            pltpu.VMEM((2, packed, cells), f32),
            pltpu.VMEM((2, packed, cells), f32),
            pltpu.VMEM((2, packed, cells), f32),
            dma((7,)),
            dma((2,)), dma((2,)), dma((2, 2)), dma((2,)), dma((2,)),
            dma((2, species)), dma((species,)), dma((tiles,)), dma((tiles,)), dma((2,)), dma((2,)), dma((2,)), dma((2,)),
        ],
        compiler_params=pltpu.CompilerParams(
            collective_id=0, has_side_effects=True, vmem_limit_bytes=24 * 1024 * 1024
        ),
    )(*(pltpu.with_memory_space_constraint(a, pltpu.HBM) for a in given))


def solution(mesh):
    placed = (
        P(None, "space", None),
        P("tm", None, "space", None),
        P(None, "space", None),
        P(),
        P(),
        P(),
    )
    return jax.shard_map(
        body,
        mesh=mesh,
        in_specs=placed,
        out_specs=P("tm", "node", None, "space", None),
        check_vma=False,
    )
```

```python
import functools

import jax
import jax.numpy as jnp
import numpy as np
from jax import lax
from jax.experimental import pallas as pl
from jax.experimental.pallas import tpu as pltpu
from jax.sharding import PartitionSpec as P

NZ = 16
WIDTH = 2
TILE = 8
GROUP = 2
LANES = 128

time_step = 0.05


def quadrature(node_count):
    points = [(position + 1.0) / node_count for position in range(node_count)]
    weights_table = np.zeros((node_count, node_count))
    for column in range(node_count):
        coeffs = [1.0]
        denominator = 1.0
        for other_node in range(node_count):
            if other_node != column:
                shifted = [0.0] + coeffs
                for degree in range(len(coeffs)):
                    shifted[degree] = shifted[degree] - points[other_node] * coeffs[degree]
                coeffs = shifted
                denominator = denominator * (points[column] - points[other_node])
        for row_node in range(node_count):
            running = 0.0
            for degree in range(len(coeffs)):
                running = running + coeffs[degree] * points[row_node] ** (degree + 1) / (degree + 1)
            weights_table[row_node, column] = running / denominator
    return (weights_table, np.array(points))


def kernel(
    slices, pieces, nodes,
    initial_hbm, forcing_hbm, decay_hbm, mix_hbm, diff_hbm, vel_hbm, out_ref,
    mix, diff, vel, start, force, decay, handed, following, grow, shift,
    coef, blend, diag, node_inv, node_add, sweep_inv, stiff, pair_inv, pair_stiff,
    field, mixed, base, given, taken, fresh,
    side_send, side_recv, edge_send, edge_first, edge_recv,
    load_sem,
    side_ss, side_rs, edge_ss, first_ss, edge_rs, start_ss, start_rs, hand_ss, hand_rs, give_ss, give_rs,
):
    species, rows, cells = following.shape
    halo = slice(rows, rows + TILE)
    h = time_step
    pieces_out = species // GROUP
    blocks = cells // LANES
    table, points = quadrature(nodes)
    n = lax.axis_index("tm")
    p = lax.axis_index("space")
    m = lax.axis_index("node")
    part_now = lax.rem(m, 2)
    partner = m + 1 - 2 * part_now
    has_left, has_right = (p > 0) | (part_now == 1), (p < pieces - 1) | (part_now == 0)
    has_before, has_after = n > 0, n < slices - 1
    left = {"space": p - 1 + part_now, "node": partner}
    right = {"space": p + part_now, "node": partner}
    sides = ((has_left, left), (has_right, right))
    step = 2 * part_now - 1
    outer = {"space": p + step, "node": partner}
    present_outer = jnp.where(part_now == 1, p < pieces - 1, p > 0)
    here = pl.ds(pl.multiple_of(TILE * part_now, TILE), TILE)
    there = pl.ds(pl.multiple_of(TILE * (1 - part_now), TILE), TILE)
    mesh_id = pl.DeviceIdType.MESH

    barrier = pltpu.get_barrier_semaphore()

    def greet(condition, where):
        @pl.when(condition)
        def _():
            pl.semaphore_signal(barrier, inc=1, device_id=where, device_id_type=mesh_id)

    greet(m >= 0, {"node": partner})
    for where in ({"tm": n - 1}, {"tm": n - 1, "node": partner}):
        greet(has_before, where)
    greet(present_outer, outer)
    greet(present_outer & has_before, {"tm": n - 1, **outer})

    load_force = pltpu.make_async_copy(forcing_hbm.at[0, :, here], force.at[:, 0:rows], load_sem.at[0])
    load_decay = pltpu.make_async_copy(decay_hbm.at[:, here], decay.at[:, 0:rows], load_sem.at[1])
    load_start = pltpu.make_async_copy(initial_hbm.at[:, here], start.at[:, 0:rows], load_sem.at[2])
    load_handed = pltpu.make_async_copy(initial_hbm.at[:, here], handed, load_sem.at[3])
    loads = [
        pltpu.make_async_copy(src, dst, load_sem.at[4 + i])
        for i, (src, dst) in enumerate([(mix_hbm, mix), (diff_hbm, diff), (vel_hbm, vel)])
    ]
    load_force.start()
    load_decay.start()
    for load in loads:
        load.start()

    @pl.when(n == 0)
    def _():
        load_start.start()
        load_handed.start()

    zero_tile = jnp.zeros((species, TILE, cells), jnp.float32)
    start[:, halo, :] = zero_tile
    force[:, halo, :] = zero_tile
    decay[:, halo, :] = zero_tile

    def send(src, dst, ss, rs, where):
        return pltpu.make_async_remote_copy(
            src_ref=src, dst_ref=dst, send_sem=ss, recv_sem=rs, device_id=where, device_id_type=mesh_id
        )

    def side_copy(k):
        return send(side_send.at[k], side_recv.at[1 - k], side_ss.at[k], side_rs.at[1 - k], sides[k][1])

    def first_copy(k):
        return send(edge_first.at[k], edge_recv.at[1 - k], first_ss.at[k], edge_rs.at[1 - k], sides[k][1])

    def edge_copy(k):
        return send(
            edge_send.at[k], edge_recv.at[1 - k], edge_ss.at[k], edge_rs.at[1 - k],
            {"tm": n + 1, **sides[k][1]},
        )

    def start_copy(c):
        group = pl.ds(GROUP * c, GROUP)
        return send(following.at[group], start.at[group, 0:rows], start_ss.at[c], start_rs.at[c], {"tm": n + 1})

    def hand_copy(q):
        group = pl.ds(q * GROUP, GROUP)
        return send(fresh.at[nodes - 1, group], handed.at[group], hand_ss.at[q], hand_rs.at[q], {"tm": n + 1})

    def give_copy(q):
        group = pl.ds(q * GROUP, GROUP)
        return send(given.at[group], taken.at[group], give_ss.at[q], give_rs.at[q], {"node": partner})

    def pack(dst, offset, src, s):
        low = offset + WIDTH * s
        dst[0, low:low + WIDTH, :] = src[s, 0:WIDTH, :]
        dst[1, low:low + WIDTH, :] = src[s, rows - WIDTH:rows, :]

    def unpack(dst, src, k, offset):
        for s in range(species):
            low = offset + WIDTH * s
            if k == 0:
                dst[s, rows + TILE - WIDTH:rows + TILE, :] = src[0, low:low + WIDTH, :]
            else:
                dst[s, rows:rows + WIDTH, :] = src[1, low:low + WIDTH, :]

    def present_count(flag):
        return flag.astype(jnp.int32)

    whole = slice(0, rows)

    def pass_on(s):
        following[s] = grow[s] * start[s, whole, :] + shift[s]

        if (s + 1) % GROUP == 0:
            @pl.when(has_after)
            def _():
                start_copy(s // GROUP).start()

        pack(edge_send, 0, following, s)

    def pass_edges():
        for k in range(2):
            @pl.when(has_after & sides[k][0])
            def _():
                edge_copy(k).start()

    beside = 1 + present_count(present_outer)
    load_force.wait()
    load_decay.wait()

    @pl.when(n == 0)
    def _():
        load_start.wait()

    pl.semaphore_wait(barrier, beside + present_count(has_after) * (1 + beside))

    for s in range(species):
        inverse = 1.0 / (1.0 + h * decay[s, whole, :])
        grow[s] = inverse
        shift[s] = h * force[s, whole, :] * inverse

        @pl.when(n == 0)
        def _():
            pass_on(s)

    @pl.when(n == 0)
    def _():
        pass_edges()
        for s in range(species):
            pack(edge_first, 0, start, s)
        for k in range(2):
            @pl.when(sides[k][0])
            def _():
                first_copy(k).start()

    for s in range(species):
        pack(side_send, 0, force, s)
        pack(side_send, WIDTH * species, decay, s)
    for k in range(2):
        @pl.when(sides[k][0])
        def _():
            side_copy(k).start()

    def node_scalars(which):
        time, weights = jnp.float32(0.0), [jnp.float32(0.0)] * nodes
        for i in range(nodes):
            time = jnp.where(which == i, jnp.float32(points[i]), time)
            weights = [jnp.where(which == i, jnp.float32(table[i, j]), weights[j]) for j in range(nodes)]
        return time, weights, time * jnp.float32(h / nodes)

    pair = [(m,) + node_scalars(m), (partner,) + node_scalars(partner)]

    for load in loads:
        load.wait()
    lane = lax.broadcasted_iota(jnp.int32, (TILE, LANES), 1)
    depth = lane % NZ
    is_first, is_last = depth == 0, depth == NZ - 1
    for s in range(species):
        dd = diff[s]
        drift = [0.5 * vel[i, s] for i in range(3)]
        for i in range(3):
            plus = jnp.full((TILE, LANES), dd - drift[i])
            minus = jnp.full((TILE, LANES), dd + drift[i])
            if i == 2:
                plus = jnp.where(is_last, 0.0, plus)
                minus = jnp.where(is_first, 0.0, minus)
            coef[s, 2 * i] = plus
            coef[s, 2 * i + 1] = minus
        for t in range(species):
            blend[s, t] = jnp.full((TILE, LANES), mix[s, t])

    def prepare(s, part):
        d = decay[s, part, :]
        f = force[s, part, :]
        diag[s, part, :] = d + 6.0 * diff[s]
        for j in range(nodes):
            inverse = 1.0 / (1.0 + float(points[j] * h) * d)
            node_inv[j, s, part, :] = inverse
            node_add[j, s, part, :] = float(points[j] * h) * f * inverse
            portion = float(h * points[j] / nodes) * d
            inverse = 1.0 / (1.0 + portion)
            sweep_inv[j, s, part, :] = inverse
            stiff[j, s, part, :] = portion * inverse

    for s in range(species):
        prepare(s, whole)
        for i in range(2):
            portion = pair[i][3] * decay[s, whole, :]
            inverse = 1.0 / (1.0 + portion)
            pair_inv[i, s] = inverse
            pair_stiff[i, s] = portion * inverse
    for k in range(2):
        @pl.when(sides[k][0])
        def _():
            side_copy(1 - k).wait_recv()
            unpack(force, side_recv, k, 0)
            unpack(decay, side_recv, k, WIDTH * species)
    for s in range(species):
        prepare(s, halo)

    def node_values(s, part):
        w = start[s, part, :]
        return [w * node_inv[j, s, part, :] + node_add[j, s, part, :] for j in range(nodes)]

    def interior_values(s):
        values = node_values(s, whole)
        for j in range(nodes):
            field[j, s, TILE:TILE + rows, :] = values[j]
            field[j, s, 2 * TILE + rows:3 * TILE + rows, :] = values[j][0:TILE]

    @pl.when(n == 0)
    def _():
        for s in range(species):
            interior_values(s)

    @pl.when(has_before)
    def _():
        for s in range(species):
            if s % GROUP == 0:
                start_copy(s // GROUP).wait_recv()
            pass_on(s)
            interior_values(s)
        pass_edges()

    for k in range(2):
        @pl.when(sides[k][0])
        def _():
            edge_copy(1 - k).wait_recv()
            unpack(start, edge_recv, k, 0)
    for s in range(species):
        values = node_values(s, halo)
        for j in range(nodes):
            field[j, s, 0:TILE, :] = values[j]
            field[j, s, TILE + rows:2 * TILE + rows, :] = values[j]

    row = lax.broadcasted_iota(jnp.int32, (TILE, LANES), 0)
    inside = ((row < WIDTH) & has_right) | ((row >= TILE - WIDTH) & has_left)
    y_up, y_down = lane < LANES - NZ, lane >= NZ
    block = [slice(LANES * b, LANES * (b + 1)) for b in range(blocks)]

    def pick(ref, s, part):
        return [ref[s, part, cut] for cut in block]

    def linear(ref, s, low, coefs, d):
        c = pick(ref, s, slice(low, low + TILE))
        x_plus = pick(ref, s, slice(low + 1, low + TILE + 1))
        x_minus = pick(ref, s, slice(low - 1, low + TILE - 1))
        up = [pltpu.roll(v, LANES - NZ, 1) for v in c]
        down = [pltpu.roll(v, NZ, 1) for v in c]
        total = []
        for b in range(blocks):
            y_plus = jnp.where(y_up, up[b], up[(b + 1) % blocks])
            y_minus = jnp.where(y_down, down[b], down[b - 1])
            total.append(
                (coefs[0] * x_plus[b] + coefs[1] * x_minus[b])
                + (coefs[2] * y_plus + coefs[3] * y_minus)
                + (coefs[4] * pltpu.roll(c[b], LANES - 1, 1) + coefs[5] * pltpu.roll(c[b], 1, 1))
                - d[b] * c[b]
            )
        return total

    def coupled(values, weights):
        result = []
        for b in range(blocks):
            total = weights[0] * values[0][b]
            for t in range(1, species):
                total = total + weights[t] * values[t][b]
            result.append(jnp.tanh(total))
        return result

    for t in range(2):
        part = slice(TILE * t, TILE * t + TILE)
        low = TILE * (t + 1)
        is_halo = t == 1
        centers = [[pick(field.at[j], s, slice(low, low + TILE)) for s in range(species)] for j in range(nodes)]
        for s in range(species):
            coefs = [coef[s, i] for i in range(6)]
            weights = [blend[s, i] for i in range(species)]
            d = pick(diag, s, part)
            f = pick(force, s, part)
            w = pick(start, s, part)
            rates = []
            for j in range(nodes):
                flow = linear(field.at[j], s, low, coefs, d)
                pull = coupled(centers[j], weights)
                rates.append([flow[b] + pull[b] + f[b] for b in range(blocks)])
            for b in range(blocks):
                sums = [0.0, 0.0]
                for i in range(nodes):
                    total = w[b]
                    for j in range(nodes):
                        total = total + float(h * table[i, j]) * rates[j][b]
                    v = total * sweep_inv[i, s, part, block[b]] + centers[i][s][b] * stiff[i, s, part, block[b]]
                    if is_halo:
                        v = jnp.where(inside, v, 0.0)
                    else:
                        fresh[i, s, part, block[b]] = v
                    sums = [sums[e] + pair[e][2][i] * v for e in range(2)]
                for e in range(2):
                    mixed[e, s, low:low + TILE, block[b]] = sums[e]
                    if is_halo:
                        mixed[e, s, 0:TILE, block[b]] = sums[e]
            if not is_halo and (s + 1) % GROUP == 0:
                @pl.when(has_after)
                def _():
                    hand_copy(s // GROUP).start()

    centers = [[pick(fresh.at[j], s, whole) for s in range(species)] for j in range(nodes)]
    for s in range(species):
        weights = [blend[s, i] for i in range(species)]
        coefs = [coef[s, i] for i in range(6)]
        d = pick(diag, s, whole)
        f = pick(force, s, whole)
        pull = [coupled(centers[j], weights) for j in range(nodes)]
        for e in range(2):
            which, time, row_weights, _ = pair[e]
            flow = linear(mixed.at[e], s, TILE, coefs, d)
            for b in range(blocks):
                total = flow[b] + time * f[b]
                own = centers[0][s][b]
                for j in range(nodes):
                    total = total + row_weights[j] * pull[j][b]
                    if j > 0:
                        own = jnp.where(which == j, centers[j][s][b], own)
                value = h * total * pair_inv[e, s, :, block[b]] + own * pair_stiff[e, s, :, block[b]]
                base[e, s, :, block[b]] = value

    @pl.when(n == 0)
    def _():
        load_handed.wait()

    for q in range(pieces_out):
        group = slice(q * GROUP, (q + 1) * GROUP)

        @pl.when(has_before)
        def _():
            hand_copy(q).wait_recv()

        given[group] = handed[group] * pair_inv[1, group] + base[1, group]
        give_copy(q).start()
        out_ref[0, 0, group, here, :] = handed[group] * pair_inv[0, group] + base[0, group]
    for q in range(pieces_out):
        group = slice(q * GROUP, (q + 1) * GROUP)
        give_copy(q).wait_recv()
        out_ref[0, 0, group, there, :] = taken[group]

    for q in range(pieces_out):
        give_copy(q).wait_send()
    for k in range(2):
        @pl.when(sides[k][0])
        def _():
            side_copy(k).wait_send()

        @pl.when(sides[k][0] & (n == 0))
        def _():
            first_copy(k).wait_send()

        @pl.when(sides[k][0] & has_after)
        def _():
            edge_copy(k).wait_send()

    @pl.when(has_after)
    def _():
        for c in range(species // GROUP):
            start_copy(c).wait_send()
        for q in range(pieces_out):
            hand_copy(q).wait_send()


def body(*given):
    initial, _, _, mixing, diffusivity, velocity = given
    slices, pieces, nodes = (lax.axis_size(a) for a in ("tm", "space", "node"))
    species, rows, cells = initial.shape
    assert rows == 2 * TILE and nodes % 2 == 0
    longer = 2 * TILE
    packed = WIDTH * species
    groups = species // GROUP
    f32 = jnp.float32
    dma = pltpu.SemaphoreType.DMA
    hbm = pl.BlockSpec(memory_space=pltpu.HBM)
    plain = pltpu.VMEM((species, TILE, cells), f32)
    twice = pltpu.VMEM((2, species, TILE, cells), f32)
    extended = pltpu.VMEM((species, longer, cells), f32)
    per_node = pltpu.VMEM((nodes, species, longer, cells), f32)
    return pl.pallas_call(
        functools.partial(kernel, slices, pieces, nodes),
        out_shape=jax.ShapeDtypeStruct((1, 1, species, rows, cells), f32),
        in_specs=[hbm] * 6,
        out_specs=pl.BlockSpec(memory_space=pltpu.VMEM),
        scratch_shapes=[
            pltpu.SMEM(mixing.shape, f32), pltpu.SMEM(diffusivity.shape, f32), pltpu.SMEM(velocity.shape, f32),
            extended, extended, extended, plain, plain, plain, plain,
            pltpu.VMEM((species, 6, TILE, LANES), f32),
            pltpu.VMEM((species, species, TILE, LANES), f32),
            extended, per_node, per_node, per_node, per_node, twice, twice,
            pltpu.VMEM((nodes, species, 4 * TILE, cells), f32),
            pltpu.VMEM((2, species, 3 * TILE, cells), f32),
            twice, plain, plain, pltpu.VMEM((nodes, species, TILE, cells), f32),
            pltpu.VMEM((2, 2 * packed, cells), f32),
            pltpu.VMEM((2, 2 * packed, cells), f32),
            pltpu.VMEM((2, packed, cells), f32),
            pltpu.VMEM((2, packed, cells), f32),
            pltpu.VMEM((2, packed, cells), f32),
            dma((7,)),
            dma((2,)), dma((2,)), dma((2,)), dma((2,)), dma((2,)),
            dma((groups,)), dma((groups,)), dma((groups,)), dma((groups,)), dma((groups,)), dma((groups,)),
        ],
        compiler_params=pltpu.CompilerParams(
            collective_id=0, has_side_effects=True, vmem_limit_bytes=24 * 1024 * 1024
        ),
    )(*(pltpu.with_memory_space_constraint(a, pltpu.HBM) for a in given))


def solution(mesh):
    placed = (
        P(None, "space", None),
        P("tm", None, "space", None),
        P(None, "space", None),
        P(),
        P(),
        P(),
    )
    return jax.shard_map(
        body,
        mesh=mesh,
        in_specs=placed,
        out_specs=P("tm", "node", None, "space", None),
        check_vma=False,
    )
```

```python
import functools

import jax
import jax.numpy as jnp
import numpy as np
from jax import lax
from jax.experimental import pallas as pl
from jax.experimental.pallas import tpu as pltpu
from jax.sharding import PartitionSpec as P

NZ = 16
WIDTH = 2
TILE = 8

time_step = 0.05


def quadrature(node_count):
    points = [(position + 1.0) / node_count for position in range(node_count)]
    weights_table = np.zeros((node_count, node_count))
    for column in range(node_count):
        coeffs = [1.0]
        denominator = 1.0
        for other_node in range(node_count):
            if other_node != column:
                shifted = [0.0] + coeffs
                for degree in range(len(coeffs)):
                    shifted[degree] = shifted[degree] - points[other_node] * coeffs[degree]
                coeffs = shifted
                denominator = denominator * (points[column] - points[other_node])
        for row_node in range(node_count):
            running = 0.0
            for degree in range(len(coeffs)):
                running = running + coeffs[degree] * points[row_node] ** (degree + 1) / (degree + 1)
            weights_table[row_node, column] = running / denominator
    return (weights_table, np.array(points))


def kernel(
    slices, pieces, nodes,
    initial_hbm, forcing_hbm, decay_hbm, mix_hbm, diff_hbm, vel_hbm, out_ref,
    mix, diff, vel, start, force, decay, handed, following, grow, shift,
    node_inv, node_add, sweep_inv, own_inv,
    field, mixed, base, last_value,
    side_send, side_recv, edge_send, edge_first, edge_recv,
    load_sem,
    side_ss, side_rs, edge_ss, first_ss, edge_rs, start_ss, start_rs, hand_ss, hand_rs,
):
    species, rows, cells = following.shape
    tiles = rows // TILE
    halo = slice(rows, rows + TILE)
    h = time_step
    table, points = quadrature(nodes)
    n = lax.axis_index("tm")
    p = lax.axis_index("space")
    m = lax.axis_index("node")
    has_left, has_right = p > 0, p < pieces - 1
    has_before, has_after = n > 0, n < slices - 1
    sides = ((has_left, p - 1), (has_right, p + 1))
    mesh_id = pl.DeviceIdType.MESH

    barrier = pltpu.get_barrier_semaphore()

    def greet(condition, where):
        @pl.when(condition)
        def _():
            pl.semaphore_signal(barrier, inc=1, device_id=where, device_id_type=mesh_id)

    greet(has_before, {"tm": n - 1})
    for present, place in sides:
        greet(present, {"space": place})
        greet(present & has_before, {"tm": n - 1, "space": place})

    load_force = pltpu.make_async_copy(forcing_hbm.at[0], force.at[:, 0:rows], load_sem.at[0])
    load_decay = pltpu.make_async_copy(decay_hbm, decay.at[:, 0:rows], load_sem.at[1])
    load_start = pltpu.make_async_copy(initial_hbm, start.at[:, 0:rows], load_sem.at[2])
    load_handed = pltpu.make_async_copy(initial_hbm, handed, load_sem.at[3])
    loads = [
        pltpu.make_async_copy(src, dst, load_sem.at[4 + i])
        for i, (src, dst) in enumerate([(mix_hbm, mix), (diff_hbm, diff), (vel_hbm, vel)])
    ]
    load_force.start()
    load_decay.start()
    for load in loads:
        load.start()

    @pl.when(n == 0)
    def _():
        load_start.start()
        load_handed.start()

    zero_tile = jnp.zeros((species, TILE, cells), jnp.float32)
    start[:, halo, :] = zero_tile
    force[:, halo, :] = zero_tile
    decay[:, halo, :] = zero_tile

    def send(src, dst, ss, rs, where):
        return pltpu.make_async_remote_copy(
            src_ref=src, dst_ref=dst, send_sem=ss, recv_sem=rs, device_id=where, device_id_type=mesh_id
        )

    def side_copy(k):
        return send(side_send.at[k], side_recv.at[1 - k], side_ss.at[k], side_rs.at[1 - k], {"space": sides[k][1]})

    def first_copy(k):
        return send(edge_first.at[k], edge_recv.at[1 - k], first_ss.at[k], edge_rs.at[1 - k], {"space": sides[k][1]})

    def edge_copy(k):
        return send(
            edge_send.at[k], edge_recv.at[1 - k], edge_ss.at[k], edge_rs.at[1 - k],
            {"tm": n + 1, "space": sides[k][1]},
        )

    def start_copy(s, t):
        part = pl.ds(TILE * t, TILE)
        return send(following.at[s, part], start.at[s, part], start_ss.at[s, t], start_rs.at[s, t], {"tm": n + 1})

    def hand_copy(t):
        part = pl.ds(TILE * t, TILE)
        return send(last_value.at[:, part], handed.at[:, part], hand_ss.at[t], hand_rs.at[t], {"tm": n + 1})

    def pack(dst, offset, src, s):
        low = offset + WIDTH * s
        dst[0, low:low + WIDTH, :] = src[s, 0:WIDTH, :]
        dst[1, low:low + WIDTH, :] = src[s, rows - WIDTH:rows, :]

    def unpack(dst, src, k, offset):
        for s in range(species):
            low = offset + WIDTH * s
            if k == 0:
                dst[s, rows + TILE - WIDTH:rows + TILE, :] = src[0, low:low + WIDTH, :]
            else:
                dst[s, rows:rows + WIDTH, :] = src[1, low:low + WIDTH, :]

    load_force.wait()
    load_decay.wait()
    whole = slice(0, rows)
    for s in range(species):
        inverse = 1.0 / (1.0 + h * decay[s, whole, :])
        grow[s] = inverse
        shift[s] = h * force[s, whole, :] * inverse
        pack(side_send, 0, force, s)
        pack(side_send, WIDTH * species, decay, s)

    def present_count(flag):
        return flag.astype(jnp.int32)

    beside = present_count(has_left) + present_count(has_right)
    pl.semaphore_wait(barrier, beside + present_count(has_after) * (1 + beside))

    def pass_on(s):
        for t in range(tiles):
            part = slice(TILE * t, TILE * t + TILE)

            @pl.when(has_before)
            def _():
                start_copy(s, t).wait_recv()

            following[s, part, :] = grow[s, part, :] * start[s, part, :] + shift[s, part, :]

            @pl.when(has_after)
            def _():
                start_copy(s, t).start()

        pack(edge_send, 0, following, s)

    def pass_edges():
        for k in range(2):
            @pl.when(has_after & sides[k][0])
            def _():
                edge_copy(k).start()

    @pl.when(n == 0)
    def _():
        load_start.wait()
        for s in range(species):
            pass_on(s)
        pass_edges()
        for s in range(species):
            pack(edge_first, 0, start, s)
        for k in range(2):
            @pl.when(sides[k][0])
            def _():
                first_copy(k).start()

    for k in range(2):
        @pl.when(sides[k][0])
        def _():
            side_copy(k).start()

    own_time = jnp.float32(0.0)
    own_row = [jnp.float32(0.0)] * nodes
    for i in range(nodes):
        own_time = jnp.where(m == i, jnp.float32(points[i]), own_time)
        own_row = [jnp.where(m == i, jnp.float32(table[i, j]), own_row[j]) for j in range(nodes)]
    own_stiff = own_time * jnp.float32(h / nodes)

    def prepare(s, part):
        d = decay[s, part, :]
        f = force[s, part, :]
        for j in range(nodes):
            inverse = 1.0 / (1.0 + float(points[j] * h) * d)
            node_inv[j, s, part, :] = inverse
            node_add[j, s, part, :] = float(points[j] * h) * f * inverse
            sweep_inv[j, s, part, :] = 1.0 / (1.0 + float(h * points[j] / nodes) * d)

    for s in range(species):
        prepare(s, whole)
        own_inv[s] = 1.0 / (1.0 + own_stiff * decay[s, whole, :])
    for k in range(2):
        @pl.when(sides[k][0])
        def _():
            side_copy(1 - k).wait_recv()
            unpack(force, side_recv, k, 0)
            unpack(decay, side_recv, k, WIDTH * species)
    for s in range(species):
        prepare(s, halo)

    def node_values(s, part):
        w = start[s, part, :]
        return [w * node_inv[j, s, part, :] + node_add[j, s, part, :] for j in range(nodes)]

    def interior_values(s):
        values = node_values(s, whole)
        for j in range(nodes):
            field[j, s, TILE:TILE + rows, :] = values[j]
            field[j, s, 2 * TILE + rows:3 * TILE + rows, :] = values[j][0:TILE]

    @pl.when(n == 0)
    def _():
        for s in range(species):
            interior_values(s)

    @pl.when(has_before)
    def _():
        for s in range(species):
            pass_on(s)
            interior_values(s)
        pass_edges()

    for k in range(2):
        @pl.when(sides[k][0])
        def _():
            edge_copy(1 - k).wait_recv()
            unpack(start, edge_recv, k, 0)
    for s in range(species):
        values = node_values(s, halo)
        for j in range(nodes):
            field[j, s, 0:TILE, :] = values[j]
            field[j, s, TILE + rows:2 * TILE + rows, :] = values[j]

    for load in loads:
        load.wait()
    depth = lax.broadcasted_iota(jnp.int32, (TILE, cells), 1) % NZ
    is_first, is_last = depth == 0, depth == NZ - 1
    row = lax.broadcasted_iota(jnp.int32, (TILE, cells), 0)
    inside = ((row < WIDTH) & has_right) | ((row >= TILE - WIDTH) & has_left)

    def linear(ref, s, low, d):
        c = ref[s, low:low + TILE, :]
        x_plus = ref[s, low + 1:low + TILE + 1, :]
        x_minus = ref[s, low - 1:low + TILE - 1, :]
        y_plus = pltpu.roll(c, cells - NZ, 1)
        y_minus = pltpu.roll(c, NZ, 1)
        z_plus = jnp.where(is_last, 0.0, pltpu.roll(c, cells - 1, 1))
        z_minus = jnp.where(is_first, 0.0, pltpu.roll(c, 1, 1))
        dd = diff[s]
        vx, vy, vz = 0.5 * vel[0, s], 0.5 * vel[1, s], 0.5 * vel[2, s]
        return (
            ((dd - vx) * x_plus + (dd + vx) * x_minus)
            + ((dd - vy) * y_plus + (dd + vy) * y_minus)
            + ((dd - vz) * z_plus + (dd + vz) * z_minus)
            - (6.0 * dd + d) * c
        )

    def coupled(values, s):
        total = mix[s, 0] * values[0]
        for t in range(1, species):
            total = total + mix[s, t] * values[t]
        return jnp.tanh(total)

    for t in list(range(tiles)) + [tiles]:
        part = slice(TILE * t, TILE * t + TILE)
        low = TILE * (t + 1)
        is_halo = t == tiles
        fresh = [[None] * species for _ in range(nodes)]
        centers = [[field[j, s, low:low + TILE, :] for s in range(species)] for j in range(nodes)]
        for s in range(species):
            d = decay[s, part, :]
            f = force[s, part, :]
            w = start[s, part, :]
            rates = [linear(field.at[j], s, low, d) + coupled(centers[j], s) + f for j in range(nodes)]
            for i in range(nodes):
                total = float(h * table[i, 0]) * rates[0]
                for j in range(1, nodes):
                    total = total + float(h * table[i, j]) * rates[j]
                v = (w + total + float(h * points[i] / nodes) * d * centers[i][s]) * sweep_inv[i, s, part, :]
                fresh[i][s] = jnp.where(inside, v, 0.0) if is_halo else v
            if not is_halo:
                last_value[s, part, :] = fresh[nodes - 1][s]
            sum_now = own_row[0] * fresh[0][s]
            for j in range(1, nodes):
                sum_now = sum_now + own_row[j] * fresh[j][s]
            mixed[s, low:low + TILE, :] = sum_now
            if is_halo:
                mixed[s, 0:TILE, :] = sum_now
        if not is_halo:
            @pl.when(has_after)
            def _():
                hand_copy(t).start()

            for s in range(species):
                gained = own_time * force[s, part, :]
                own = fresh[0][s]
                for j in range(nodes):
                    gained = gained + own_row[j] * coupled(fresh[j], s)
                    if j > 0:
                        own = jnp.where(m == j, fresh[j][s], own)
                base[s, part, :] = h * gained + own_stiff * decay[s, part, :] * own

    for t in range(tiles):
        part = slice(TILE * t, TILE * t + TILE)
        for s in range(species):
            rate = linear(mixed, s, TILE * (t + 1), decay[s, part, :])
            base[s, part, :] = (base[s, part, :] + h * rate) * own_inv[s, part, :]

    @pl.when(n == 0)
    def _():
        load_handed.wait()

    for t in range(tiles):
        part = slice(TILE * t, TILE * t + TILE)

        @pl.when(has_before)
        def _():
            hand_copy(t).wait_recv()

        out_ref[0, 0, :, part, :] = handed[:, part, :] * own_inv[:, part, :] + base[:, part, :]

    for k in range(2):
        @pl.when(sides[k][0])
        def _():
            side_copy(k).wait_send()

        @pl.when(sides[k][0] & (n == 0))
        def _():
            first_copy(k).wait_send()

        @pl.when(sides[k][0] & has_after)
        def _():
            edge_copy(k).wait_send()

    @pl.when(has_after)
    def _():
        for s in range(species):
            for t in range(tiles):
                start_copy(s, t).wait_send()
        for t in range(tiles):
            hand_copy(t).wait_send()


def body(*given):
    initial, _, _, mixing, diffusivity, velocity = given
    slices, pieces, nodes = (lax.axis_size(a) for a in ("tm", "space", "node"))
    species, rows, cells = initial.shape
    longer = rows + TILE
    packed = WIDTH * species
    tiles = rows // TILE
    f32 = jnp.float32
    dma = pltpu.SemaphoreType.DMA
    hbm = pl.BlockSpec(memory_space=pltpu.HBM)
    plain = pltpu.VMEM((species, rows, cells), f32)
    extended = pltpu.VMEM((species, longer, cells), f32)
    per_node = pltpu.VMEM((nodes, species, longer, cells), f32)
    return pl.pallas_call(
        functools.partial(kernel, slices, pieces, nodes),
        out_shape=jax.ShapeDtypeStruct((1, 1, species, rows, cells), f32),
        in_specs=[hbm] * 6,
        out_specs=pl.BlockSpec(memory_space=pltpu.VMEM),
        scratch_shapes=[
            pltpu.SMEM(mixing.shape, f32), pltpu.SMEM(diffusivity.shape, f32), pltpu.SMEM(velocity.shape, f32),
            extended, extended, extended, plain, plain, plain, plain,
            per_node, per_node, per_node, plain,
            pltpu.VMEM((nodes, species, rows + 3 * TILE, cells), f32),
            pltpu.VMEM((species, rows + 2 * TILE, cells), f32),
            plain, plain,
            pltpu.VMEM((2, 2 * packed, cells), f32),
            pltpu.VMEM((2, 2 * packed, cells), f32),
            pltpu.VMEM((2, packed, cells), f32),
            pltpu.VMEM((2, packed, cells), f32),
            pltpu.VMEM((2, packed, cells), f32),
            dma((7,)),
            dma((2,)), dma((2,)), dma((2,)), dma((2,)), dma((2,)),
            dma((species, tiles)), dma((species, tiles)), dma((tiles,)), dma((tiles,)),
        ],
        compiler_params=pltpu.CompilerParams(
            collective_id=0, has_side_effects=True, vmem_limit_bytes=24 * 1024 * 1024
        ),
    )(*(pltpu.with_memory_space_constraint(a, pltpu.HBM) for a in given))


def solution(mesh):
    placed = (
        P(None, "space", None),
        P("tm", None, "space", None),
        P(None, "space", None),
        P(),
        P(),
        P(),
    )
    return jax.shard_map(
        body,
        mesh=mesh,
        in_specs=placed,
        out_specs=P("tm", "node", None, "space", None),
        check_vma=False,
    )
```
